32 devices in a mesh: ctx: 8 (over y, x, core), head: 4 (over z).
Axes of the slice: x: 2, y: 2, z: 4, core: 2. Of those that a mesh axis runs over, the one named last changes fastest.
Arguments:
- mixed_in: bfloat16 [2048, 8192], P(('ctx', 'head')), may hold values from -6 to 6
- conv_weight: float32 [4, 8192], P(None, 'head'), may hold values from -3 to 3
- write_strength_logit: float32 [32, 2048], P('head', 'ctx'), may hold values from -10.5 to 2.2, as said below
- decay_log: float32 [32, 2048], P('head', 'ctx'), may hold values from -0.7 to 0, as said below
- initial_state: float32 [32, 128, 128], P('head'), may hold values from -6 to 6
- final_state_grad: float32 [32, 128, 128], P('head'), may hold values from -6 to 6
- grad_out: bfloat16 [2048, 4096], P('ctx', 'head'), may hold values from -6 to 6
Outputs:
- grad_mixed: bfloat16 [2048, 8192], P(('ctx', 'head'))
- grad_conv: float32 [4, 8192], P(None, 'head')
- grad_beta_logit: float32 [32, 2048], P('head', 'ctx')
- grad_decay_log: float32 [32, 2048], P('head', 'ctx')
The draws below stay inside these ranges and needn't reach their ends.
Inputs may be any that keep to these rules, and one draw needn't show every extreme that they name: `write_strength_logit`: each value head's write strengths and decays vary from token to token. `decay_log`: every entry is negative.
All inputs are finite; a program needn't handle non-finite values.
Results may differ from the reference program's by a relative error of at most 0.001.
Values may be sent and summed in bfloat16 or wider, within the bound.
No kernel may reach another device: no remote copies, remote signals or barrier semaphores. Data moves between devices by JAX's collectives and lax.ppermute only.
A program may use at most 128 MiB of HBM per device.

```python
import math
import jax
import jax.numpy as jnp
from jax import lax

HK = 16
VALUE_HEADS = 32
DK = 128
DV = 128
KW = 4
BLOCK = 64
SLAB_TOKENS = 2048
CH = 8192


def keeping_heads(key):
    share = 0.5
    return jax.random.uniform(jax.random.fold_in(key, 7), (VALUE_HEADS, 1)) < share


def roughness(key):
    return jnp.exp(jax.random.uniform(key, (VALUE_HEADS, SLAB_TOKENS), minval=-0.7, maxval=0.7))


def draw_write_strength_logit(key, part):
    keeping = keeping_heads(key)
    first = jax.random.fold_in(key, 11)
    second = jax.random.fold_in(key, 12)
    level = jnp.exp(jax.random.uniform(first, (VALUE_HEADS, 1), minval=math.log(0.05), maxval=math.log(0.5)))
    strength = jnp.where(keeping, level * DK / SLAB_TOKENS, level)
    strength = jnp.minimum(strength * roughness(second), 0.9)
    return (jnp.log(strength) - jnp.log1p(-strength)).astype(jnp.float32)


def draw_decay_log(key, part):
    keeping = keeping_heads(key)
    first = jax.random.fold_in(key, 21)
    second = jax.random.fold_in(key, 22)
    third = jax.random.fold_in(key, 23)
    fourth = jax.random.fold_in(key, 24)
    fifth_piece = jax.random.fold_in(key, 25)
    slow_rate = jnp.exp(jax.random.uniform(first, (VALUE_HEADS, 1), minval=math.log(0.02), maxval=math.log(0.3))) / SLAB_TOKENS
    fast_rate = 1.0 / jax.random.uniform(second, (VALUE_HEADS, 1), minval=30.0, maxval=50.0)
    rate = jnp.where(keeping, slow_rate, fast_rate)
    smoothed_signal = -rate * roughness(third)
    spots = jax.random.randint(fourth, (VALUE_HEADS, 3, 1), 0, SLAB_TOKENS)
    positions = jnp.arange(SLAB_TOKENS, dtype=jnp.int32)[None, None, :]
    matched_entry = jnp.any(positions == spots, axis=1)
    sudden_spike = jnp.log(jax.random.uniform(fifth_piece, (VALUE_HEADS, SLAB_TOKENS), minval=0.5, maxval=0.8))
    return jnp.where(matched_entry, sudden_spike, smoothed_signal).astype(jnp.float32)


def block_scale(rng, dims, cuts, least, top_value):
    level = 1.0
    for dim, shards_of in cuts:
        draws = jax.random.uniform(jax.random.fold_in(jax.random.fold_in(rng, 6), dim), (shards_of,), jnp.float32, least / len(cuts), top_value / len(cuts))
        level = level * jnp.repeat(jnp.exp(draws), dims[dim] // shards_of).reshape((-1,) + (1,) * (len(dims) - 1 - dim))
    return level


def normal_values(key, extent, scale, reach, cuts=(), held_as=jnp.bfloat16):
    loudness = block_scale(key, extent, cuts, -0.22, 0.18) if cuts else 1.0
    entries = jax.random.normal(key, extent, jnp.float32) * scale * loudness
    return jnp.minimum(jnp.maximum(entries, -reach), reach).astype(held_as)


def setup_inputs(seed: int = 0) -> dict:
    arg_keys = jax.random.split(jax.random.key(seed), 8)
    mixed_in = normal_values(arg_keys[0], (SLAB_TOKENS, CH), 1.0, 6.0, ((0, 32),))
    conv_weight = normal_values(arg_keys[1], (KW, CH), KW ** -0.5, 3.0, ((1, 4),), jnp.float32)
    write_strength_logit = draw_write_strength_logit(jax.random.fold_in(arg_keys[7], 71), 0)
    decay_log = draw_decay_log(jax.random.fold_in(arg_keys[7], 71), 0)
    initial_state = normal_values(arg_keys[4], (VALUE_HEADS, DK, DV), 1.0, 6.0, ((0, 4),), jnp.float32)
    final_state_grad = normal_values(arg_keys[5], (VALUE_HEADS, DK, DV), 1.0, 6.0, ((0, 4),), jnp.float32)
    grad_out = normal_values(arg_keys[6], (SLAB_TOKENS, VALUE_HEADS * DV), 1.0, 6.0, ((0, 8), (1, 4)))
    return {"mixed_in": mixed_in, "conv_weight": conv_weight, "write_strength_logit": write_strength_logit, "decay_log": decay_log, "initial_state": initial_state, "final_state_grad": final_state_grad, "grad_out": grad_out}


highest = lax.Precision.HIGHEST
norm_eps = 1e-06

def block_step(carried, pieces):
    state, transit = carried
    queries, key_feats, values, beta_gate, log_decay = pieces
    block_size = log_decay.shape[0]
    cumulative = jnp.cumsum(log_decay)
    row_ids = lax.broadcasted_iota(jnp.int32, (block_size, block_size), 0)
    col_ids = lax.broadcasted_iota(jnp.int32, (block_size, block_size), 1)
    causal = col_ids <= row_ids
    differ = jnp.where(causal, cumulative[:, None] - cumulative[None, :], 0.0)
    ratios = jnp.where(causal, jnp.exp(differ), 0.0)
    key_gram = jnp.dot(key_feats, key_feats.T, precision=highest)
    lower_part = jnp.where(col_ids < row_ids, beta_gate[:, None] * ratios * key_gram, 0.0)
    system = lower_part + jnp.eye(block_size, dtype=jnp.float32)
    decays = jnp.exp(cumulative)
    right_sides = jnp.concatenate([beta_gate[:, None] * values, (beta_gate * decays)[:, None] * key_feats], axis=1)
    solved = jax.scipy.linalg.solve_triangular(system, right_sides, lower=True)
    width_v = values.shape[1]
    base_update = solved[:, :width_v]
    weights = solved[:, width_v:]
    update = base_update - jnp.dot(weights, state, precision=highest)
    scores = ratios * jnp.dot(queries, key_feats.T, precision=highest)
    output = decays[:, None] * jnp.dot(queries, state, precision=highest) + jnp.dot(scores, update, precision=highest)
    total_decay = jnp.exp(cumulative[-1])
    tail_keys = jnp.exp(cumulative[-1] - cumulative)[:, None] * key_feats
    new_state = total_decay * state + jnp.dot(tail_keys.T, update, precision=highest)
    step_map = total_decay * jnp.eye(key_feats.shape[1], dtype=jnp.float32) - jnp.dot(tail_keys.T, weights, precision=highest)
    new_transit = jnp.dot(step_map, transit, precision=highest)
    return ((new_state, new_transit), output)

def run_head(state, queries, key_feats, values, beta_gate, log_decay):
    blocks = queries.shape[0] // BLOCK
    pieces = (queries.reshape(blocks, BLOCK, -1), key_feats.reshape(blocks, BLOCK, -1), values.reshape(blocks, BLOCK, -1), beta_gate.reshape(blocks, BLOCK), log_decay.reshape(blocks, BLOCK))
    start = (state, jnp.eye(key_feats.shape[1], dtype=jnp.float32))
    (state_end, transit), outputs = lax.scan(jax.checkpoint(block_step), start, pieces)
    return (outputs.reshape(-1, values.shape[1]), state_end, transit)

def normalize(feats, factor):
    return feats * lax.rsqrt(lax.optimization_barrier(jnp.sum(feats * feats, axis=-1, keepdims=True)) + norm_eps) * factor

def mix_layer(state_in, extended, conv_weight, write_strength_logit, decay_log):
    row_count = extended.shape[0] - (KW - 1)
    filtered_signal = conv_weight[0] * extended[0:row_count]
    for tap in range(1, KW):
        filtered_signal = filtered_signal + conv_weight[tap] * extended[tap:tap + row_count]
    activated = jax.nn.silu(filtered_signal)
    ratio_heads = VALUE_HEADS // HK
    group_width = 2 * DK + ratio_heads * DV
    groups = activated.reshape(row_count, -1, group_width)
    key_heads = groups.shape[1]
    queries = normalize(groups[:, :, :DK], DK ** (-0.5))
    key_feats = normalize(groups[:, :, DK:2 * DK], 1.0)
    values = groups[:, :, 2 * DK:].reshape(row_count, key_heads * ratio_heads, DV).transpose(1, 0, 2)
    queries = jnp.repeat(queries.transpose(1, 0, 2), ratio_heads, axis=0)
    key_feats = jnp.repeat(key_feats.transpose(1, 0, 2), ratio_heads, axis=0)
    beta_gate = jax.nn.sigmoid(write_strength_logit)
    outputs, state_out, transit = jax.vmap(run_head)(state_in, queries, key_feats, values, beta_gate, decay_log)
    result = outputs.transpose(1, 0, 2).reshape(row_count, -1)
    return ((result, state_out), transit)

def reference(mixed_in, conv_weight, write_strength_logit, decay_log, initial_state, final_state_grad, grad_out):
    extended = jnp.concatenate([jnp.zeros((KW - 1, mixed_in.shape[1]), jnp.float32), mixed_in.astype(jnp.float32)], axis=0)

    def forward(ext_rows, weight_taps, logits, decay_logs):
        return mix_layer(initial_state, ext_rows, weight_taps, logits, decay_logs)
    primal, pull_all, transit = jax.vjp(forward, extended, conv_weight, write_strength_logit, decay_log, has_aux=True)
    grads = pull_all((grad_out.astype(jnp.float32), final_state_grad))
    return (grads[0][KW - 1:].astype(jnp.bfloat16), grads[1], grads[2], grads[3])
```

```python
import functools
import jax
import jax.numpy as jnp
from jax import lax
from jax.experimental import pallas as pl
from jax.experimental.pallas import tpu as pltpu
from jax.sharding import PartitionSpec as P

HK = 16
VALUE_HEADS = 32
DK = 128
DV = 128
KW = 4
RATIO = VALUE_HEADS // HK
GROUP = 2 * DK + RATIO * DV
TILE = 128
BASE = 8
HALO = 16
EDGE = 8

norm_eps = 1e-06
f32 = jnp.float32
bf16 = jnp.bfloat16
NN = (((1,), (0,)), ((), ()))
NT = (((1,), (1,)), ((), ()))


def split(a):
    high = a.astype(bf16)
    return (high, (a - high.astype(f32)).astype(bf16))


def mm(a, b, dims=NN):
    total = lax.dot_general(a[0], b[0], dims, preferred_element_type=f32)
    if len(b) > 1:
        total += lax.dot_general(a[0], b[1], dims, preferred_element_type=f32)
    if len(a) > 1:
        total += lax.dot_general(a[1], b[0], dims, preferred_element_type=f32)
    return total


def iotas(rows, cols):
    return (
        lax.broadcasted_iota(jnp.int32, (rows, cols), 0),
        lax.broadcasted_iota(jnp.int32, (rows, cols), 1),
    )


def tile_inverses(lowers):
    row, col = iotas(TILE, TILE)
    eye = jnp.where(row == col, 1.0, 0.0).astype(f32)
    width = BASE
    same = row // width == col // width
    powers = [jnp.where(same, -low, 0.0) for low in lowers]
    inverses = [eye + p for p in powers]
    reach = 2
    while reach < BASE:
        parts = [split(p) for p in powers]
        powers = [mm(p, p) for p in parts]
        parts = [split(p) for p in powers]
        inverses = [inv + mm(split(inv), p) for inv, p in zip(inverses, parts)]
        reach *= 2
    while width < TILE:
        same = row // width == col // width
        wider = row // (2 * width) == col // (2 * width)
        between = wider & jnp.logical_not(same)
        parts = [split(inv) for inv in inverses]
        inner = [
            mm(split(jnp.where(between, low, 0.0)), inv) for low, inv in zip(lowers, parts)
        ]
        inverses = [inv - mm(p, split(i)) for inv, p, i in zip(inverses, parts, inner)]
        width *= 2
    return inverses


def unit_lower_inverses(lowers):
    size = lowers[0].shape[0]
    if size == TILE:
        return tile_inverses(lowers)
    half = size // 2
    inverses = unit_lower_inverses(
        [low[:half, :half] for low in lowers] + [low[half:, half:] for low in lowers]
    )
    first, second = (inverses[: len(lowers)], inverses[len(lowers) :])
    inner = [mm(split(low[half:, :half]), split(inv)) for low, inv in zip(lowers, first)]
    below = [-mm(split(inv), split(i)) for inv, i in zip(second, inner)]
    zero = jnp.zeros((half, half), f32)
    return [
        jnp.concatenate(
            [jnp.concatenate([a, zero], axis=1), jnp.concatenate([c, b], axis=1)], axis=0
        )
        for a, b, c in zip(first, second, below)
    ]


def sigmoid(a):
    return 1.0 / (1.0 + jnp.exp(-a))


def unit_rows(a):
    scale = lax.rsqrt(jnp.sum(a * a, axis=-1, keepdims=True) + norm_eps)
    return (a * scale, scale)


def local_kernel(x_ref, halo_ref, w_ref, rows_ref, cols_ref, do_ref, conv_ref, saved_ref, maps_ref, ext):
    tokens = x_ref.shape[0]
    ext[:HALO] = halo_ref[...].astype(f32)
    ext[HALO:] = x_ref[...].astype(f32)
    start = HALO - (KW - 1)
    conv = w_ref[0:1] * ext[start : start + tokens]
    for tap in range(1, KW):
        conv += w_ref[tap : tap + 1] * ext[start + tap : start + tap + tokens]
    conv_ref[...] = conv
    act = conv * sigmoid(conv)
    q = unit_rows(act[:, :DK])[0] * DK**-0.5
    k = unit_rows(act[:, DK : 2 * DK])[0]
    qs, ks = (split(q), split(k))
    gram = mm(ks, ks, NT)
    kq = mm(ks, qs, NT)
    qt = split(q.T)
    kt = split(k.T)
    row, col = iotas(tokens, tokens)
    lowers = []
    for h in range(RATIO):
        cum_r, cum_c = (rows_ref[0, h : h + 1], cols_ref[0, :, h : h + 1])
        beta = cols_ref[0, :, RATIO + h : RATIO + h + 1]
        ratio = jnp.exp(jnp.minimum(cum_c - cum_r, 0.0))
        lowers.append(jnp.where(col < row, beta * ratio * gram, 0.0))
    inverses = unit_lower_inverses(lowers)
    for h in range(RATIO):
        cum_r, cum_c = (rows_ref[0, h : h + 1], cols_ref[0, :, h : h + 1])
        beta = cols_ref[0, :, RATIO + h : RATIO + h + 1]
        gamma = jnp.exp(cum_c)
        total = cum_c[tokens - 1 :]
        tail = jnp.exp(total - cum_c)
        v = act[:, 2 * DK + h * DV : 2 * DK + (h + 1) * DV]
        do = do_ref[:, h * DV : (h + 1) * DV]
        right = jnp.concatenate([beta * v, (beta * gamma) * k], axis=1)
        solved = mm(split(inverses[h]), split(right))
        scores_t = jnp.where(col >= row, jnp.exp(jnp.minimum(cum_r - cum_c, 0.0)) * kq, 0.0)
        du = mm(split(scores_t), (do,))
        pulled = mm(split(inverses[h].T), split(jnp.concatenate([du, tail * k], axis=1)))
        saved_ref[h, :, : DV + DK] = solved
        saved_ref[h, :, DV + DK :] = pulled
        packed = jnp.concatenate([tail * solved, (beta * gamma) * pulled[:, :DV]], axis=1)
        moved = mm(kt, split(packed))
        drow, dcol = iotas(DK, DK)
        maps_ref[h, 0] = jnp.where(drow == dcol, jnp.exp(total), 0.0) - moved[:, DV : DV + DK]
        maps_ref[h, 1] = moved[:, :DV]
        maps_ref[h, 2] = mm(qt, split(gamma * do.astype(f32))) - moved[:, DV + DK :]


def scan_kernel(maps_ref, first_ref, last_ref, out_ref):
    count = maps_ref.shape[0]
    state, adjoint = (first_ref[0], last_ref[0])
    for step in range(count):
        back = count - 1 - step
        out_ref[step, 0, 0] = state
        out_ref[back, 0, 1] = adjoint
        if step < count - 1:
            state = mm(split(maps_ref[step, 0, 0]), split(state)) + maps_ref[step, 0, 1]
            adjoint = mm(split(maps_ref[back, 0, 0].T), split(adjoint)) + maps_ref[back, 0, 2]


def grad_kernel(
    x_ref, halo_ref, w_ref, rows_ref, cols_ref, do_ref, conv_ref, saved_ref, ends_ref,
    own_ref, edge_ref, spill_ref, dw_ref, drows_ref, dcols_ref, ext, dext,
):
    tokens = x_ref.shape[0]
    conv = conv_ref[...]
    gate = sigmoid(conv)
    act = conv * gate
    qn, q_scale = unit_rows(act[:, :DK])
    q = qn * DK**-0.5
    k, k_scale = unit_rows(act[:, DK : 2 * DK])
    qs, ks = (split(q), split(k))
    gram = mm(ks, ks, NT)
    scores = mm(qs, ks, NT)
    row, col = iotas(tokens, tokens)
    dq, dk = (jnp.zeros((tokens, DK), f32), jnp.zeros((tokens, DK), f32))
    dscores, dgram = (jnp.zeros((tokens, tokens), f32), jnp.zeros((tokens, tokens), f32))
    dvs = []
    drows, dcols = ([], [])
    for h in range(RATIO):
        cum_r, cum_c = (rows_ref[0, h : h + 1], cols_ref[0, :, h : h + 1])
        beta = cols_ref[0, :, RATIO + h : RATIO + h + 1]
        gamma = jnp.exp(cum_c)
        total = cum_c[tokens - 1 :]
        tail = jnp.exp(total - cum_c)
        ratio = jnp.exp(jnp.minimum(cum_c - cum_r, 0.0))
        v = act[:, 2 * DK + h * DV : 2 * DK + (h + 1) * DV]
        do = (do_ref[:, h * DV : (h + 1) * DV],)
        state, adjoint = (ends_ref[h, 0], ends_ref[h, 1])
        ss, ds = (split(state), split(adjoint))
        u = saved_ref[h, :, :DV] - mm(split(saved_ref[h, :, DV : DV + DK]), ss)
        z = saved_ref[h, :, DV + DK : 2 * DV + DK] + mm(
            split(saved_ref[h, :, 2 * DV + DK :]), ds
        )
        us, zs = (split(u), split(z))
        dq_in = mm(do, ss, NT)
        dk_in = -mm(zs, ss, NT)
        dk_out = mm(us, ds, NT)
        score_part = jnp.where(col <= row, mm(do, us, NT) * ratio, 0.0)
        gram_part = jnp.where(col < row, mm(zs, us, NT) * -ratio, 0.0)
        gram_term = gram_part * gram
        dscores += score_part
        dgram += beta * gram_part
        both = beta * gram_term + score_part * scores
        gate_in = gamma * jnp.sum(dk_in * k, axis=1, keepdims=True)
        dbeta = jnp.sum(gram_term, axis=1, keepdims=True) + gate_in
        dbeta += jnp.sum(z * v, axis=1, keepdims=True)
        dvs.append(beta * z)
        dq += gamma * dq_in
        dk += (beta * gamma) * dk_in + tail * dk_out
        left = tail * jnp.sum(dk_out * k, axis=1, keepdims=True)
        dcum = jnp.sum(both, axis=1, keepdims=True) - left + beta * gate_in
        dcum += gamma * jnp.sum(dq_in * q, axis=1, keepdims=True)
        at_end = jnp.sum(left, axis=0, keepdims=True) + jnp.exp(total) * jnp.sum(
            jnp.sum(state * adjoint, axis=1, keepdims=True), axis=0, keepdims=True
        )
        last = lax.broadcasted_iota(jnp.int32, (tokens, 1), 0) == tokens - 1
        dcum += jnp.where(last, at_end, 0.0)
        dcols.append((dcum, dbeta))
        drows.append(jnp.sum(both, axis=0, keepdims=True))
    dss, dgs = (split(dscores), split(dgram + dgram.T))
    dq += mm(dss, ks)
    dk += mm(split(dscores.T), qs) + mm(dgs, ks)
    lane = lax.broadcasted_iota(jnp.int32, (tokens, 8), 1)
    packed = jnp.zeros((tokens, 8), f32)
    for h in range(RATIO):
        packed = jnp.where(lane == h, dcols[h][0], packed)
        packed = jnp.where(lane == RATIO + h, dcols[h][1], packed)
    dcols_ref[0] = packed
    drows_ref[0] = jnp.concatenate(drows + [jnp.zeros((8 - RATIO, tokens), f32)], axis=0)
    dqn = dq * DK**-0.5
    dq_raw = q_scale * (dqn - qn * jnp.sum(qn * dqn, axis=1, keepdims=True))
    dk_raw = k_scale * (dk - k * jnp.sum(k * dk, axis=1, keepdims=True))
    dact = jnp.concatenate([dq_raw, dk_raw] + dvs, axis=1)
    dconv = dact * (gate * (1.0 + conv * (1.0 - gate)))
    ext[:HALO] = halo_ref[...].astype(f32)
    ext[HALO:] = x_ref[...].astype(f32)
    start = HALO - (KW - 1)
    for tap in range(KW):
        dw_ref[tap : tap + 1] = jnp.sum(
            dconv * ext[start + tap : start + tap + tokens], axis=0, keepdims=True
        )
    zero = jnp.zeros((EDGE, GROUP), f32)
    dext[:EDGE] = zero
    dext[EDGE : EDGE + tokens] = dconv
    dext[EDGE + tokens :] = zero
    own = jnp.zeros((tokens, GROUP), f32)
    spill = jnp.zeros((EDGE, GROUP), f32)
    for tap in range(KW):
        begin = EDGE + KW - 1 - tap
        own += w_ref[tap : tap + 1] * dext[begin : begin + tokens]
        begin = KW - 1 - tap
        spill += w_ref[tap : tap + 1] * dext[begin : begin + EDGE]
    own_ref[...] = own.astype(bf16)
    edge_ref[...] = own[tokens - EDGE :]
    spill_ref[...] = spill


def params():
    return pltpu.CompilerParams(vmem_limit_bytes=48 * 1024 * 1024)


def from_behind(value, axis, by):
    devices = lax.axis_size(axis)
    pairs = [(i, i + by) for i in range(devices) if 0 <= i + by < devices]
    return lax.ppermute(value, axis, pairs)


def shape(*dims, dtype=f32):
    return jax.ShapeDtypeStruct(dims, dtype)


def local_pass(x, halo, weight, rows, cols, do):
    tokens, feats = x.shape
    groups = feats // GROUP
    heads = groups * RATIO
    width = 2 * (DV + DK)
    return pl.pallas_call(
        local_kernel,
        grid=(groups,),
        in_specs=[
            pl.BlockSpec((tokens, GROUP), lambda g: (0, g)),
            pl.BlockSpec((HALO, GROUP), lambda g: (0, g)),
            pl.BlockSpec((KW, GROUP), lambda g: (0, g)),
            pl.BlockSpec((1, 8, tokens), lambda g: (g, 0, 0)),
            pl.BlockSpec((1, tokens, 8), lambda g: (g, 0, 0)),
            pl.BlockSpec((tokens, RATIO * DV), lambda g: (0, g)),
        ],
        out_specs=[
            pl.BlockSpec((tokens, GROUP), lambda g: (0, g)),
            pl.BlockSpec((RATIO, tokens, width), lambda g: (g, 0, 0)),
            pl.BlockSpec((RATIO, 3, DK, DV), lambda g: (g, 0, 0, 0)),
        ],
        out_shape=[
            shape(tokens, feats),
            shape(heads, tokens, width),
            shape(heads, 3, DK, DV),
        ],
        scratch_shapes=[pltpu.VMEM((HALO + tokens, GROUP), f32)],
        compiler_params=params(),
        name="local_pass",
    )(x, halo, weight, rows, cols, do)


def scan_pass(maps, first, last):
    count, heads = maps.shape[:2]
    return pl.pallas_call(
        scan_kernel,
        grid=(heads,),
        in_specs=[
            pl.BlockSpec((count, 1, 3, DK, DV), lambda h: (0, h, 0, 0, 0)),
            pl.BlockSpec((1, DK, DV), lambda h: (h, 0, 0)),
            pl.BlockSpec((1, DK, DV), lambda h: (h, 0, 0)),
        ],
        out_specs=pl.BlockSpec((count, 1, 2, DK, DV), lambda h: (0, h, 0, 0, 0)),
        out_shape=shape(count, heads, 2, DK, DV),
        compiler_params=params(),
        name="scan_pass",
    )(maps, first, last)


def grad_pass(x, halo, weight, rows, cols, do, conv, saved, ends):
    tokens, feats = x.shape
    groups = feats // GROUP
    width = saved.shape[-1]
    return pl.pallas_call(
        grad_kernel,
        grid=(groups,),
        in_specs=[
            pl.BlockSpec((tokens, GROUP), lambda g: (0, g)),
            pl.BlockSpec((HALO, GROUP), lambda g: (0, g)),
            pl.BlockSpec((KW, GROUP), lambda g: (0, g)),
            pl.BlockSpec((1, 8, tokens), lambda g: (g, 0, 0)),
            pl.BlockSpec((1, tokens, 8), lambda g: (g, 0, 0)),
            pl.BlockSpec((tokens, RATIO * DV), lambda g: (0, g)),
            pl.BlockSpec((tokens, GROUP), lambda g: (0, g)),
            pl.BlockSpec((RATIO, tokens, width), lambda g: (g, 0, 0)),
            pl.BlockSpec((RATIO, 2, DK, DV), lambda g: (g, 0, 0, 0)),
        ],
        out_specs=[
            pl.BlockSpec((tokens, GROUP), lambda g: (0, g)),
            pl.BlockSpec((EDGE, GROUP), lambda g: (0, g)),
            pl.BlockSpec((EDGE, GROUP), lambda g: (0, g)),
            pl.BlockSpec((KW, GROUP), lambda g: (0, g)),
            pl.BlockSpec((1, 8, tokens), lambda g: (g, 0, 0)),
            pl.BlockSpec((1, tokens, 8), lambda g: (g, 0, 0)),
        ],
        out_shape=[
            shape(tokens, feats, dtype=bf16),
            shape(EDGE, feats),
            shape(EDGE, feats),
            shape(KW, feats),
            shape(groups, 8, tokens),
            shape(groups, tokens, 8),
        ],
        scratch_shapes=[
            pltpu.VMEM((HALO + tokens, GROUP), f32),
            pltpu.VMEM((tokens + 2 * EDGE, GROUP), f32),
        ],
        compiler_params=params(),
        name="grad_pass",
    )(x, halo, weight, rows, cols, do, conv, saved, ends)


def cross_blocks(maps, first, last):
    devices, mine = (lax.axis_size("ctx"), lax.axis_index("ctx"))
    heads = maps.shape[0]
    if heads % devices == 0:
        share = heads // devices
        maps = lax.all_to_all(maps, "ctx", split_axis=0, concat_axis=0, tiled=True)
        maps = maps.reshape(devices, share, 3, DK, DV)
        first = lax.dynamic_slice_in_dim(first, mine * share, share, 0)
        last = lax.dynamic_slice_in_dim(last, mine * share, share, 0)
        ends = scan_pass(maps, first, last).reshape(heads, 2, DK, DV)
        return lax.all_to_all(ends, "ctx", split_axis=0, concat_axis=0, tiled=True)
    ends = scan_pass(lax.all_gather(maps, "ctx"), first, last)
    return lax.dynamic_index_in_dim(ends, mine, 0, keepdims=False)


def on_device(
    mixed_in,
    conv_weight,
    write_strength_logit,
    decay_log,
    initial_state,
    final_state_grad,
    grad_out,
):
    heads, tokens = decay_log.shape
    groups = heads // RATIO
    beta = jax.nn.sigmoid(write_strength_logit)
    cumulative = jnp.cumsum(decay_log, axis=1)
    rows = jnp.concatenate(
        [
            cumulative.reshape(groups, RATIO, tokens),
            beta.reshape(groups, RATIO, tokens),
            jnp.zeros((groups, 8 - 2 * RATIO, tokens), f32),
        ],
        axis=1,
    )
    cols = rows.transpose(0, 2, 1)
    x = lax.all_to_all(mixed_in, "head", split_axis=1, concat_axis=0, tiled=True)
    halo = from_behind(x[-HALO:], "ctx", 1)
    conv, saved, maps = local_pass(x, halo, conv_weight, rows, cols, grad_out)
    ends = cross_blocks(maps, initial_state, final_state_grad)
    own, edge, spill, dweight, drows, dcols = grad_pass(
        x, halo, conv_weight, rows, cols, grad_out, conv, saved, ends
    )
    spilled = from_behind(spill[EDGE - (KW - 1) :], "ctx", -1)
    last_rows = (edge[EDGE - (KW - 1) :] + spilled).astype(bf16)
    own = jnp.concatenate([own[: -(KW - 1)], last_rows], axis=0)
    returned = lax.all_to_all(own, "head", split_axis=0, concat_axis=1, tiled=True)
    weight_total = lax.psum(dweight, "ctx")
    dcum = dcols[:, :, :RATIO].transpose(0, 2, 1) - drows[:, :RATIO]
    dcum = dcum.reshape(heads, tokens)
    grad_decay = lax.cumsum(dcum, axis=1, reverse=True)
    dbeta = dcols[:, :, RATIO : 2 * RATIO].transpose(0, 2, 1).reshape(heads, tokens)
    grad_beta = dbeta * beta * (1.0 - beta)
    return (returned, weight_total, grad_beta, grad_decay)


def solution(mesh):
    in_specs = (
        P(("ctx", "head"), None),
        P(None, "head"),
        P("head", "ctx"),
        P("head", "ctx"),
        P("head", None, None),
        P("head", None, None),
        P("ctx", "head"),
    )
    out_specs = (P(("ctx", "head"), None), P(None, "head"), P("head", "ctx"), P("head", "ctx"))
    return jax.shard_map(
        on_device, mesh=mesh, in_specs=in_specs, out_specs=out_specs, check_vma=False
    )
```

```python
import functools
import jax
import jax.numpy as jnp
from jax import lax
from jax.experimental import pallas as pl
from jax.experimental.pallas import tpu as pltpu
from jax.sharding import PartitionSpec as P

HK = 16
VALUE_HEADS = 32
DK = 128
DV = 128
KW = 4
RATIO = VALUE_HEADS // HK
GROUP = 2 * DK + RATIO * DV
TILE = 128
BASE = 2
EDGE = 16
VMEM_BYTES = 24 * 1024 * 1024

norm_eps = 1e-06
f32 = jnp.float32
bf16 = jnp.bfloat16
NN = (((1,), (0,)), ((), ()))
NT = (((1,), (1,)), ((), ()))


def split(a):
    high = a.astype(bf16)
    return (high, (a - high.astype(f32)).astype(bf16))


def dot(a, b, dims):
    return lax.dot_general(a, b, dims, preferred_element_type=f32)


def mm(a, b, dims=NN):
    inner_axis = dims[0][1][0]
    inner, outer = (b[0].shape[inner_axis], b[0].shape[1 - inner_axis])
    if len(b) == 1:
        return dot(a[0], b[0], dims) + dot(a[1], b[0], dims)
    high, low = b
    exact = len(a) == 1
    if outer <= TILE:
        wide = jnp.concatenate([high, low], axis=1 - inner_axis)
        if exact:
            total = dot(a[0], wide, dims)
        elif inner <= TILE:
            both = jnp.concatenate([wide, wide], axis=inner_axis)
            total = dot(jnp.concatenate(a, axis=1), both, dims)
        else:
            total = dot(a[0], wide, dims) + dot(a[1], wide, dims)
        return total[:, :outer] + total[:, outer:]
    if inner <= TILE:
        if exact:
            deep = jnp.concatenate([high, low], axis=inner_axis)
            return dot(jnp.concatenate([a[0], a[0]], axis=1), deep, dims)
        deep = jnp.concatenate([high, high], axis=inner_axis)
        return dot(jnp.concatenate(a, axis=1), deep, dims) + dot(a[0], low, dims)
    total = dot(a[0], high, dims) + dot(a[0], low, dims)
    return total if exact else total + dot(a[1], high, dims)


def iotas(rows, cols):
    return (
        lax.broadcasted_iota(jnp.int32, (rows, cols), 0),
        lax.broadcasted_iota(jnp.int32, (rows, cols), 1),
    )


def tile_inverses(lowers):
    row, col = iotas(TILE, TILE)
    eye = jnp.where(row == col, 1.0, 0.0).astype(f32)
    width = BASE
    same = row // width == col // width
    inverses = [eye - jnp.where(same, low, 0.0) for low in lowers]
    while width < TILE:
        same = row // width == col // width
        wider = row // (2 * width) == col // (2 * width)
        between = wider & jnp.logical_not(same)
        parts = [split(inv) for inv in inverses]
        inner = [
            mm(split(jnp.where(between, low, 0.0)), inv) for low, inv in zip(lowers, parts)
        ]
        inverses = [inv - mm(p, split(i)) for inv, p, i in zip(inverses, parts, inner)]
        width *= 2
    return inverses


def unit_lower_inverses(lowers):
    size = lowers[0].shape[0]
    if size == TILE:
        return tile_inverses(lowers)
    half = size // 2
    inverses = unit_lower_inverses(
        [low[:half, :half] for low in lowers] + [low[half:, half:] for low in lowers]
    )
    first, second = (inverses[: len(lowers)], inverses[len(lowers) :])
    inner = [mm(split(low[half:, :half]), split(inv)) for low, inv in zip(lowers, first)]
    below = [-mm(split(inv), split(i)) for inv, i in zip(second, inner)]
    zero = jnp.zeros((half, half), f32)
    return [
        jnp.concatenate(
            [jnp.concatenate([a, zero], axis=1), jnp.concatenate([c, b], axis=1)], axis=0
        )
        for a, b, c in zip(first, second, below)
    ]


def sigmoid(a):
    return 1.0 / (1.0 + jnp.exp(-a))


def unit_rows(a):
    scale = lax.rsqrt(jnp.sum(a * a, axis=-1, keepdims=True) + norm_eps)
    return (a * scale, scale)


def prefix_sums(a):
    count, size = a.shape
    high, low = split(a)
    rest = (a - high.astype(f32) - low.astype(f32)).astype(bf16)
    row, col = iotas(size, size)
    parts = dot(
        jnp.concatenate([high, low, rest], axis=0), jnp.where(row <= col, 1.0, 0.0).astype(bf16), NN
    )
    return parts[:count] + parts[count : 2 * count] + parts[2 * count :]


def gates_kernel(logit_ref, decay_ref, causal_ref, gates_ref, beta_ref):
    heads, tokens = decay_ref.shape
    row, col = iotas(tokens, tokens)
    cum = prefix_sums(decay_ref[...])
    beta = sigmoid(logit_ref[...])
    beta_ref[...] = beta
    cols = jnp.concatenate([cum, beta], axis=0).T
    for g in range(heads // RATIO):
        first = g * RATIO
        for h in range(first, first + RATIO):
            ratio = jnp.exp(jnp.minimum(cols[:, h : h + 1] - cum[h : h + 1], 0.0))
            causal_ref[h] = jnp.where(col <= row, ratio, 0.0)
        cum_c = cols[:, first : first + RATIO]
        gates_ref[g, :, :RATIO] = cols[:, heads + first : heads + first + RATIO]
        gates_ref[g, :, RATIO : 2 * RATIO] = jnp.exp(cum_c)
        gates_ref[g, :, 2 * RATIO : 3 * RATIO] = jnp.exp(cum_c[tokens - 1 :] - cum_c)


def wide_gates(gates_ref, group, h):
    tokens = gates_ref.shape[1]
    cols = [gates_ref[group, :, i * RATIO + h : i * RATIO + h + 1] for i in range(3)]
    return [jnp.broadcast_to(c, (tokens, DK)) for c in cols]


def group_at(place_ref, slot):
    first, flip = slot
    return first if flip is None else first + ((place_ref[1] & 1) ^ flip)


def lanes(start, size):
    return pl.ds(start if isinstance(start, int) else pl.multiple_of(start, size), size)


def local_kernel(slots, place_ref, mixed_ref, *refs):
    each = len(slots)
    outs, exts = (refs[-6 * each : -each], refs[-each:])
    groups = [group_at(place_ref, slot) for slot in slots]
    lowers = []
    for at, group in enumerate(groups):
        lowers += group_system(
            group, place_ref, mixed_ref, refs[: -6 * each], *outs[at : 3 * each : each], exts[at]
        )
    inverses = unit_lower_inverses(lowers)
    for at, group in enumerate(groups):
        group_maps(
            group, inverses[at * RATIO : (at + 1) * RATIO], refs[: -6 * each], *outs[each + at :: each]
        )


def group_system(group, place_ref, mixed_ref, refs, x_out, act_ref, slope_ref, ext):
    *piece_refs, halo_ref, w_ref, causal_ref, gates_in, do_ref = refs
    mine = place_ref[0]
    here = lanes(group * GROUP, GROUP)
    count = mixed_ref.shape[0]
    pieces = len(piece_refs) + 1
    tokens = pieces * count
    feats = mixed_ref.shape[1] // pieces
    ext[:EDGE] = halo_ref[:, here].astype(f32)
    x_out[:EDGE] = halo_ref[:, here]
    for s in range(pieces):
        if s == 0:
            piece = mixed_ref[:, pl.ds(pl.multiple_of(mine * feats + group * GROUP, GROUP), GROUP)]
        else:
            piece = piece_refs[s - 1][:, here]
        begin = pl.multiple_of(EDGE + (mine ^ s) * count, EDGE)
        ext[pl.ds(begin, count)] = piece.astype(f32)
        x_out[pl.ds(begin, count)] = piece
    start = EDGE - (KW - 1)
    conv = w_ref[0:1, here] * ext[start : start + tokens]
    for tap in range(1, KW):
        conv += w_ref[tap : tap + 1, here] * ext[start + tap : start + tap + tokens]
    gate = sigmoid(conv)
    act = conv * gate
    slope = gate + act * (1.0 - gate)
    qn, q_scale = unit_rows(act[:, :DK])
    k, k_scale = unit_rows(act[:, DK : 2 * DK])
    act_ref[:, :DK] = qn
    act_ref[:, DK : 2 * DK] = k
    act_ref[:, 2 * DK :] = act[:, 2 * DK :]
    slope_ref[:, :DK] = slope[:, :DK] * q_scale
    slope_ref[:, DK : 2 * DK] = slope[:, DK : 2 * DK] * k_scale
    slope_ref[:, 2 * DK :] = slope[:, 2 * DK :]
    ks = split(k)
    gram = mm(ks, ks, NT)
    row, col = iotas(tokens, tokens)
    gram = jnp.where(col < row, gram, 0.0)
    lowers = []
    for h in range(RATIO):
        beta = wide_gates(gates_in, group, h)[0]
        wide = jnp.concatenate([beta] * (tokens // DK), axis=1)
        lowers.append(causal_ref[group * RATIO + h] * gram * wide)
    return lowers


def group_maps(group, inverses, refs, act_ref, slope_ref, saved_ref, maps_ref):
    *_, causal_ref, gates_in, do_ref = refs
    tokens = act_ref.shape[0]
    q = act_ref[:, :DK] * DK**-0.5
    k = act_ref[:, DK : 2 * DK]
    scores = mm(split(q), split(k), NT)
    qt = split(q.T)
    kt = split(k.T)
    for h in range(RATIO):
        head = group * RATIO + h
        beta, gamma, tail = wide_gates(gates_in, group, h)
        beta_gamma = beta * gamma
        v = act_ref[:, 2 * DK + h * DV : 2 * DK + (h + 1) * DV]
        do = do_ref[:, lanes(head * DV, DV)]
        solved = mm(split(inverses[h]), split(jnp.concatenate([beta * v, beta_gamma * k], axis=1)))
        du = mm(split((causal_ref[head] * scores).T), (do,))
        pulled = mm(split(inverses[h].T), split(jnp.concatenate([du, tail * k], axis=1)))
        saved_ref[h, :, : DV + DK] = solved
        saved_ref[h, :, DV + DK :] = pulled
        packed = [tail * solved[:, :DV], tail * solved[:, DV:], beta_gamma * pulled[:, :DV]]
        moved = mm(kt, split(jnp.concatenate(packed, axis=1)))
        drow, dcol = iotas(DK, DK)
        total = gamma[tokens - 1 :]
        maps_ref[h, 0] = jnp.where(drow == dcol, total, 0.0) - moved[:, DV : DV + DK]
        maps_ref[h, 1] = moved[:, :DV]
        maps_ref[h, 2] = mm(qt, split(gamma * do.astype(f32))) - moved[:, DV + DK :]


def ordered(core, own, other):
    return (jnp.where(core == 0, own, other), jnp.where(core == 0, other, own))


def compose_kernel(parts, place_ref, *refs):
    keeps, others, outs, held = (refs[:parts], refs[parts : 2 * parts], refs[2 * parts : -1], refs[-1])
    core, chip = (place_ref[1] & 1, place_ref[1] >> 1)
    share = keeps[0].shape[0]
    for p in range(parts):
        for i in range(share):
            maps0, maps1 = ordered(core, keeps[p][i], others[p][i])
            later = mm(split(maps1[0]), split(jnp.concatenate([maps0[0], maps0[1]], axis=1)))
            held[p * share + i, 0] = later[:, :DK]
            held[p * share + i, 1] = later[:, DK:] + maps1[1]
            held[p * share + i, 2] = mm(split(maps0[0].T), split(maps1[2])) + maps0[2]
    for s, out in enumerate(outs):
        out[...] = held[chip ^ s]


def chips_kernel(chips, place_ref, *refs):
    maps_refs, first_ref, last_ref, outs, held, ends = (
        refs[:chips], refs[chips], refs[chips + 1], refs[chips + 2 : -2], refs[-2], refs[-1],
    )
    chip = place_ref[1] >> 1
    for s, maps_ref in enumerate(maps_refs):
        held[chip ^ s] = maps_ref[...]
    share = RATIO
    head = (chip // share * 2 + (place_ref[1] & 1)) * share + chip % share
    state, adjoint = (first_ref[head], last_ref[head])
    for step in range(chips):
        back = chips - 1 - step
        ends[step, 0] = state
        ends[back, 1] = adjoint
        if step < chips - 1:
            state = mm(split(held[step, 0]), split(state)) + held[step, 1]
            adjoint = mm(split(held[back, 0].T), split(adjoint)) + held[back, 2]
    for s, out in enumerate(outs):
        out[...] = ends[chip ^ s]


def expand_kernel(chips, place_ref, *refs):
    ends_refs, refs = (refs[:chips], refs[chips:])
    *maps_refs, own_out, give_out, ends = refs
    parts = len(maps_refs) // 2
    keeps, others = (maps_refs[:parts], maps_refs[parts:])
    core, chip = (place_ref[1] & 1, place_ref[1] >> 1)
    for s, ends_ref in enumerate(ends_refs):
        ends[chip ^ s] = ends_ref[...]
    share = keeps[0].shape[0]
    for p in range(parts):
        for i in range(share):
            head = p * share + i
            state, adjoint = (ends[head, 0], ends[head, 1])
            maps0, maps1 = ordered(core, keeps[p][i], others[p][i])
            state1 = mm(split(maps0[0]), split(state)) + maps0[1]
            adjoint0 = mm(split(maps1[0].T), split(adjoint)) + maps1[2]
            own_out[head, 0], give_out[head, 0] = ordered(core, state, state1)
            own_out[head, 1], give_out[head, 1] = ordered(core, adjoint0, adjoint)


def scan_kernel(maps_ref, first_ref, last_ref, out_ref):
    count = maps_ref.shape[0]
    state, adjoint = (first_ref[0], last_ref[0])
    for step in range(count):
        back = count - 1 - step
        out_ref[step, 0, 0] = state
        out_ref[back, 0, 1] = adjoint
        if step < count - 1:
            state = mm(split(maps_ref[step, 0, 0]), split(state)) + maps_ref[step, 0, 1]
            adjoint = mm(split(maps_ref[back, 0, 0].T), split(adjoint)) + maps_ref[back, 0, 2]


def row_sums(a):
    return dot(jnp.ones((8, 2 * DK), bf16), jnp.concatenate(split(a), axis=1), NT)[:1]


def wide_row_sums(a):
    return dot(jnp.concatenate(split(a), axis=1), jnp.ones((2 * DK, DK), bf16), NN)


def grad_kernel(slots, sides, place_ref, *refs):
    each = len(slots)
    w_ref, beta_ref, causal_ref, gates_in, do_ref, *refs = refs
    ends_refs, refs = (refs[:sides], refs[sides:])
    kept, (*out_refs, extra_ref, gates_ref, dext, ext) = (refs[: 4 * each], refs[4 * each :])
    for at, slot in enumerate(slots):
        side, first = divmod(at * RATIO, each * RATIO // sides)
        group_grads(
            group_at(place_ref, slot), at, place_ref[0], *kept[4 * at : 4 * at + 4], w_ref, beta_ref,
            causal_ref, gates_in, do_ref, ends_refs[side].at[pl.ds(first, RATIO)], out_refs,
            extra_ref, gates_ref, dext, ext,
        )


def group_grads(
    group, at, mine, x_ref, act_ref, slope_ref, saved_ref, w_ref, beta_ref, causal_ref, gates_in,
    do_ref, ends_ref, out_refs, extra_ref, gates_ref, dext, ext,
):
    tokens = act_ref.shape[0]
    here = lanes(group * GROUP, GROUP)
    there = slice(at * GROUP, (at + 1) * GROUP)
    qn = act_ref[:, :DK]
    q = qn * DK**-0.5
    k = act_ref[:, DK : 2 * DK]
    qs, ks = (split(q), split(k))
    gram = mm(ks, ks, NT)
    scores = mm(qs, ks, NT)
    row, col = iotas(tokens, tokens)
    below = col < row
    suffix = jnp.where(row >= col, 1.0, 0.0).astype(bf16)
    dq, dk = (jnp.zeros((tokens, DK), f32), jnp.zeros((tokens, DK), f32))
    dscores, dgram = (jnp.zeros((tokens, tokens), f32), jnp.zeros((tokens, tokens), f32))
    dvs = []
    for h in range(RATIO):
        head = group * RATIO + h
        beta, gamma, tail = wide_gates(gates_in, group, h)
        v = act_ref[:, 2 * DK + h * DV : 2 * DK + (h + 1) * DV]
        do = (do_ref[:, lanes(head * DV, DV)],)
        state, adjoint = (ends_ref[h, 0], ends_ref[h, 1])
        ss, ds = (split(state), split(adjoint))
        u = saved_ref[h, :, :DV] - mm(split(saved_ref[h, :, DV : DV + DK]), ss)
        z = saved_ref[h, :, DV + DK : 2 * DV + DK] + mm(
            split(saved_ref[h, :, 2 * DV + DK :]), ds
        )
        dv = beta * z
        us, zs = (split(u), split(dv))
        dq_in = gamma * mm(do, ss, NT)
        dk_in = gamma * mm(zs, ss, NT)
        dk_out = tail * mm(us, ds, NT)
        causal = causal_ref[head]
        score_part = mm(do, us, NT) * causal
        gram_part = jnp.where(below, mm(zs, us, NT) * causal, 0.0)
        dscores += score_part
        dgram -= gram_part
        gram_term = gram_part * gram
        both = score_part * scores - gram_term
        dvs.append(dv)
        dq += dq_in
        dk += dk_out - dk_in
        key_in = dk_in * k
        left = dk_out * k
        parts = both[:, :DK]
        terms = gram_term[:, :DK]
        for begin in range(DK, tokens, DK):
            parts += both[:, begin : begin + DK]
            terms += gram_term[:, begin : begin + DK]
        dcum = row_sums(parts + dq_in * q - key_in - left) - jnp.sum(both, axis=0, keepdims=True)
        high, low = split(dcum)
        rest = (dcum - high.astype(f32) - low.astype(f32)).astype(bf16)
        stack = [high, low, rest, high, low, rest, high, low]
        summed = dot(jnp.concatenate(stack, axis=0), suffix, NN)
        at_end = jnp.sum(left, axis=0, keepdims=True) + gamma[tokens - 1 :] * jnp.sum(
            state * adjoint, axis=0, keepdims=True
        )
        gates_ref[at, h : h + 1] = (
            summed[0:1] + summed[1:2] + summed[2:3] + jnp.sum(at_end, axis=1, keepdims=True)
        )
        closed = 1.0 - beta_ref[pl.ds(head, 1)]
        gates_ref[at, RATIO + h : RATIO + h + 1] = closed * row_sums(dv * v - terms - key_in)
    dss, dgs = (split(dscores), split(dgram + dgram.T))
    dq += mm(dss, ks)
    dk += mm(split(dscores.T), qs) + mm(dgs, ks)
    dq *= DK**-0.5
    dconv = jnp.concatenate(
        [dq - qn * wide_row_sums(qn * dq), dk - k * wide_row_sums(k * dk)] + dvs, axis=1
    )
    dconv *= slope_ref[...]
    ext[...] = x_ref[...].astype(f32)
    start = EDGE - (KW - 1)
    for tap in range(KW):
        extra_ref[2 * EDGE + tap : 2 * EDGE + tap + 1, there] = jnp.sum(
            dconv * ext[start + tap : start + tap + tokens], axis=0, keepdims=True
        )
    zero = jnp.zeros((EDGE, GROUP), f32)
    dext[:EDGE] = zero
    dext[EDGE : EDGE + tokens] = dconv
    dext[EDGE + tokens :] = zero
    own = jnp.zeros((tokens, GROUP), f32)
    spill = jnp.zeros((EDGE, GROUP), f32)
    for tap in range(KW):
        begin = EDGE + KW - 1 - tap
        own += w_ref[tap : tap + 1, here] * dext[begin : begin + tokens]
        begin = KW - 1 - tap
        spill += w_ref[tap : tap + 1, here] * dext[begin : begin + EDGE]
    ext[:tokens] = own
    count = tokens // len(out_refs)
    for s, out_ref in enumerate(out_refs):
        begin = pl.multiple_of((mine ^ s) * count, EDGE)
        out_ref[:, there] = ext[pl.ds(begin, count)].astype(bf16)
    extra_ref[:EDGE, there] = own[tokens - EDGE :]
    extra_ref[EDGE : 2 * EDGE, there] = spill


def finish_kernel(slots, place_ref, extra_ref, gates_ref, *outs):
    edge_ref, spill_ref, dw_ref, decay_ref, beta_ref = outs
    for at, slot in enumerate(slots):
        group = group_at(place_ref, slot)
        here = lanes(group * GROUP, GROUP)
        there = slice(at * GROUP, (at + 1) * GROUP)
        edge_ref[:, here] = extra_ref[:EDGE, there]
        spill_ref[:, here] = extra_ref[EDGE : 2 * EDGE, there]
        dw_ref[:, here] = extra_ref[2 * EDGE :, there]
        for h in range(RATIO):
            decay_ref[pl.ds(group * RATIO + h, 1)] = gates_ref[at, h : h + 1]
            beta_ref[pl.ds(group * RATIO + h, 1)] = gates_ref[at, RATIO + h : RATIO + h + 1]


def pack_kernel(place_ref, mixed_ref, *outs):
    feats = mixed_ref.shape[1] // (len(outs) + 1)
    for s, out in enumerate(outs):
        out[...] = mixed_ref[:, lanes((place_ref[0] ^ (s + 1)) * feats, feats)]


def assemble_kernel(slots, place_ref, *refs):
    *refs, out_ref = refs
    pieces = len(refs) // 2
    rows = out_ref.shape[0]
    feats = out_ref.shape[1] // pieces
    for at, slot in enumerate(slots):
        for s in range(pieces):
            begin = (place_ref[0] ^ s) * feats + group_at(place_ref, slot) * GROUP
            out_ref[:, lanes(begin, GROUP)] = refs[s][:, at * GROUP : (at + 1) * GROUP]

    @pl.when(place_ref[0] == pieces - 1)
    def fix():
        for s in range(pieces):
            out_ref[rows - EDGE :, s * feats : (s + 1) * feats] = refs[pieces + s][...]


def shape(*dims, dtype=f32):
    return jax.ShapeDtypeStruct(dims, dtype)


def call(kernel, name, out_shape, place, args, scratch=(), flops=0):
    in_specs = [pl.BlockSpec(memory_space=pltpu.VMEM)] * len(args)
    if place is not None:
        in_specs = [pl.BlockSpec(memory_space=pltpu.SMEM)] + in_specs
        args = [place, *args]
    return pl.pallas_call(
        kernel,
        in_specs=in_specs,
        out_specs=jax.tree.map(lambda _: pl.BlockSpec(memory_space=pltpu.VMEM), out_shape),
        out_shape=out_shape,
        scratch_shapes=scratch,
        compiler_params=pltpu.CompilerParams(vmem_limit_bytes=VMEM_BYTES),
        cost_estimate=pl.CostEstimate(flops=flops, bytes_accessed=1 << 20, transcendentals=0),
        name=name,
    )(*args)


def from_behind(value, axis, by):
    devices = lax.axis_size(axis)
    pairs = [(i, i + by) for i in range(devices) if 0 <= i + by < devices]
    return lax.ppermute(value, axis, pairs)


def across(value, axis, by):
    return lax.ppermute(value, axis, [(i, i ^ by) for i in range(lax.axis_size(axis))])


def local_pass(place, slots, mixed_in, received, halo, weight, gates, do):
    tokens = gates[0].shape[1]
    each = len(slots)
    outs = call(
        functools.partial(local_kernel, slots),
        "local_pass",
        [shape(EDGE + tokens, GROUP, dtype=bf16)] * each
        + [shape(tokens, GROUP)] * (2 * each)
        + [shape(RATIO, tokens, 2 * (DV + DK))] * each
        + [shape(RATIO, 3, DK, DV)] * each,
        place,
        [mixed_in, *received, halo, weight, *gates, do],
        [pltpu.VMEM((EDGE + tokens, GROUP), f32)] * each,
        flops=each * 6 * 10**9,
    )
    kept = [outs[at : 4 * each : each] for at in range(each)]
    return (kept, outs[4 * each :])


def grad_pass(place, slots, kept, ends, weight, beta, gates, do, pieces):
    tokens = do.shape[0]
    each = len(slots)
    outs = call(
        functools.partial(grad_kernel, slots, len(ends)),
        "grad_pass",
        [shape(tokens // pieces, each * GROUP, dtype=bf16)] * pieces
        + [shape(2 * EDGE + KW, each * GROUP), shape(each, 2 * RATIO, tokens)],
        place,
        [weight, beta, *gates, do, *ends, *[a for part in kept for a in part]],
        [pltpu.VMEM((tokens + 2 * EDGE, GROUP), f32), pltpu.VMEM((tokens + EDGE, GROUP), f32)],
        flops=each * 4 * 10**9,
    )
    return (outs[:pieces], *outs[pieces:])


def scan_pass(maps, first, last):
    count, heads = maps.shape[:2]
    return pl.pallas_call(
        scan_kernel,
        grid=(heads,),
        in_specs=[
            pl.BlockSpec((count, 1, 3, DK, DV), lambda h: (0, h, 0, 0, 0)),
            pl.BlockSpec((1, DK, DV), lambda h: (h, 0, 0)),
            pl.BlockSpec((1, DK, DV), lambda h: (h, 0, 0)),
        ],
        out_specs=pl.BlockSpec((count, 1, 2, DK, DV), lambda h: (0, h, 0, 0, 0)),
        out_shape=shape(count, heads, 2, DK, DV),
        compiler_params=pltpu.CompilerParams(vmem_limit_bytes=4 * VMEM_BYTES),
        name="scan_pass",
    )(maps, first, last)


def cross_chips(place, keeps, others, initial_state, final_state_grad):
    parts = len(keeps)
    chips = parts * keeps[0].shape[0]
    joined = call(
        functools.partial(compose_kernel, parts),
        "join_cores",
        [shape(3, DK, DV)] * chips,
        place,
        [*keeps, *others],
        [pltpu.VMEM((chips, 3, DK, DV), f32)],
    )
    held = [joined[0]] + [across(joined[s], "ctx", 2 * s) for s in range(1, chips)]
    ends = call(
        functools.partial(chips_kernel, chips),
        "over_chips",
        [shape(2, DK, DV)] * chips,
        place,
        [*held, initial_state, final_state_grad],
        [pltpu.VMEM((chips, 3, DK, DV), f32), pltpu.VMEM((chips, 2, DK, DV), f32)],
    )
    ends = [ends[0]] + [across(ends[s], "ctx", 2 * s) for s in range(1, chips)]
    own, give = call(
        functools.partial(expand_kernel, chips),
        "within_chip",
        [shape(chips, 2, DK, DV)] * 2,
        place,
        [*ends, *keeps, *others],
        [pltpu.VMEM((chips, 2, DK, DV), f32)],
    )
    return (own, across(give, "ctx", 1))


def on_device(
    mixed_in,
    conv_weight,
    write_strength_logit,
    decay_log,
    initial_state,
    final_state_grad,
    grad_out,
):
    devices, pieces = (lax.axis_size("ctx"), lax.axis_size("head"))
    heads, tokens = decay_log.shape
    groups = heads // RATIO
    feats = groups * GROUP
    paired = heads == devices and groups == 4
    slots = tuple((g, None) for g in range(groups))
    if paired:
        slots = tuple((g, flip) for flip in (1, 0) for g in range(0, groups, 2))
    place = jnp.stack([lax.axis_index("head"), lax.axis_index("ctx")]).astype(jnp.int32)
    packed = call(
        pack_kernel,
        "pack",
        [shape(mixed_in.shape[0], feats, dtype=bf16)] * (pieces - 1),
        place,
        [mixed_in],
    )
    arrived = [across(piece, "head", s + 1) for s, piece in enumerate(packed)]
    mine = lax.axis_index("head")
    edge_rows = mixed_in[mixed_in.shape[0] - EDGE :, feats * (pieces - 1) :]
    for s, piece in enumerate(arrived):
        edge_rows = jnp.where((mine ^ (s + 1)) == pieces - 1, piece[piece.shape[0] - EDGE :], edge_rows)
    halo = from_behind(edge_rows, "ctx", 1)
    *gates, beta = call(
        gates_kernel,
        "gates_pass",
        [shape(heads, tokens, tokens), shape(groups, tokens, 8), shape(heads, tokens)],
        None,
        [write_strength_logit, decay_log],
    )
    kept, maps = local_pass(
        place, slots, mixed_in, arrived, halo, conv_weight, gates, grad_out
    )
    if paired:
        others = [across(part, "ctx", 1) for part in maps[: groups // 2]]
        own_ends, other_ends = cross_chips(
            place, maps[groups // 2 :], others, initial_state, final_state_grad
        )
        ends = [other_ends, own_ends]
    else:
        gathered = lax.all_gather(jnp.concatenate(maps), "ctx")
        gathered = scan_pass(gathered, initial_state, final_state_grad)
        ends = [lax.dynamic_index_in_dim(gathered, lax.axis_index("ctx"), 0, keepdims=False)]
    out_pieces, extra, gate_grad = grad_pass(
        place, slots, kept, ends, conv_weight, beta, gates, grad_out, pieces
    )
    received = [out_pieces[0]] + [across(out_pieces[s], "head", s) for s in range(1, pieces)]
    edge, spill, dweight, grad_decay, grad_beta = call(
        functools.partial(finish_kernel, slots),
        "finish",
        [
            shape(EDGE, feats),
            shape(EDGE, feats),
            shape(KW, feats),
            shape(heads, tokens),
            shape(heads, tokens),
        ],
        place,
        [extra, gate_grad],
    )
    last = (edge + from_behind(spill, "ctx", -1)).astype(bf16)
    last_rows = [
        lax.ppermute(
            last, ("ctx", "head"), [(c * pieces + h, (c + 1) * pieces - 1) for c in range(devices)]
        )
        for h in range(pieces - 1)
    ] + [last]
    returned = call(
        functools.partial(assemble_kernel, slots),
        "assemble",
        shape(mixed_in.shape[0], feats * pieces, dtype=bf16),
        place,
        [*received, *last_rows],
    )
    if devices & (devices - 1) == 0:
        by = 1
        while by < devices:
            dweight = dweight + across(dweight, "ctx", by)
            by *= 2
    else:
        dweight = lax.psum(dweight, "ctx")
    return (returned, dweight, grad_beta, grad_decay)


def solution(mesh):
    in_specs = (
        P(("ctx", "head"), None),
        P(None, "head"),
        P("head", "ctx"),
        P("head", "ctx"),
        P("head", None, None),
        P("head", None, None),
        P("ctx", "head"),
    )
    out_specs = (P(("ctx", "head"), None), P(None, "head"), P("head", "ctx"), P("head", "ctx"))
    return jax.shard_map(
        on_device, mesh=mesh, in_specs=in_specs, out_specs=out_specs, check_vma=False
    )
```

```python
import functools
import jax
import jax.numpy as jnp
from jax import lax
from jax.experimental import pallas as pl
from jax.experimental.pallas import tpu as pltpu
from jax.sharding import PartitionSpec as P

HK = 16
VALUE_HEADS = 32
DK = 128
DV = 128
KW = 4
RATIO = VALUE_HEADS // HK
GROUP = 2 * DK + RATIO * DV
TILE = 128
BASE = 2
EDGE = 16
VMEM_BYTES = 24 * 1024 * 1024

norm_eps = 1e-06
f32 = jnp.float32
bf16 = jnp.bfloat16
NN = (((1,), (0,)), ((), ()))
NT = (((1,), (1,)), ((), ()))


def split(a):
    high = a.astype(bf16)
    return (high, (a - high.astype(f32)).astype(bf16))


def dot(a, b, dims):
    return lax.dot_general(a, b, dims, preferred_element_type=f32)


def mm(a, b, dims=NN):
    inner_axis = dims[0][1][0]
    inner, outer = (b[0].shape[inner_axis], b[0].shape[1 - inner_axis])
    if len(b) == 1:
        return dot(a[0], b[0], dims) + dot(a[1], b[0], dims)
    high, low = b
    exact = len(a) == 1
    if outer <= TILE:
        wide = jnp.concatenate([high, low], axis=1 - inner_axis)
        if exact:
            total = dot(a[0], wide, dims)
        elif inner <= TILE:
            both = jnp.concatenate([wide, wide], axis=inner_axis)
            total = dot(jnp.concatenate(a, axis=1), both, dims)
        else:
            total = dot(a[0], wide, dims) + dot(a[1], wide, dims)
        return total[:, :outer] + total[:, outer:]
    if inner <= TILE:
        if exact:
            deep = jnp.concatenate([high, low], axis=inner_axis)
            return dot(jnp.concatenate([a[0], a[0]], axis=1), deep, dims)
        deep = jnp.concatenate([high, high], axis=inner_axis)
        return dot(jnp.concatenate(a, axis=1), deep, dims) + dot(a[0], low, dims)
    total = dot(a[0], high, dims) + dot(a[0], low, dims)
    return total if exact else total + dot(a[1], high, dims)


def iotas(rows, cols):
    return (
        lax.broadcasted_iota(jnp.int32, (rows, cols), 0),
        lax.broadcasted_iota(jnp.int32, (rows, cols), 1),
    )


def tile_inverses(lowers):
    row, col = iotas(TILE, TILE)
    eye = jnp.where(row == col, 1.0, 0.0).astype(f32)
    width = BASE
    same = row // width == col // width
    inverses = [eye - jnp.where(same, low, 0.0) for low in lowers]
    while width < TILE:
        same = row // width == col // width
        wider = row // (2 * width) == col // (2 * width)
        between = wider & jnp.logical_not(same)
        parts = [split(inv) for inv in inverses]
        inner = [
            mm(split(jnp.where(between, low, 0.0)), inv) for low, inv in zip(lowers, parts)
        ]
        inverses = [inv - mm(p, split(i)) for inv, p, i in zip(inverses, parts, inner)]
        width *= 2
    return inverses


def unit_lower_inverses(lowers):
    size = lowers[0].shape[0]
    if size == TILE:
        return tile_inverses(lowers)
    half = size // 2
    inverses = unit_lower_inverses(
        [low[:half, :half] for low in lowers] + [low[half:, half:] for low in lowers]
    )
    first, second = (inverses[: len(lowers)], inverses[len(lowers) :])
    inner = [mm(split(low[half:, :half]), split(inv)) for low, inv in zip(lowers, first)]
    below = [-mm(split(inv), split(i)) for inv, i in zip(second, inner)]
    zero = jnp.zeros((half, half), f32)
    return [
        jnp.concatenate(
            [jnp.concatenate([a, zero], axis=1), jnp.concatenate([c, b], axis=1)], axis=0
        )
        for a, b, c in zip(first, second, below)
    ]


def sigmoid(a):
    return 1.0 / (1.0 + jnp.exp(-a))


def unit_rows(a):
    scale = lax.rsqrt(jnp.sum(a * a, axis=-1, keepdims=True) + norm_eps)
    return (a * scale, scale)


def prefix_sums(a):
    count, size = a.shape
    high, low = split(a)
    rest = (a - high.astype(f32) - low.astype(f32)).astype(bf16)
    row, col = iotas(size, size)
    parts = dot(
        jnp.concatenate([high, low, rest], axis=0), jnp.where(row <= col, 1.0, 0.0).astype(bf16), NN
    )
    return parts[:count] + parts[count : 2 * count] + parts[2 * count :]


def gates_kernel(
    place_ref, logit_ref, decay_ref, mixed_ref, w_ref, do_ref,
    causal_ref, gates_ref, beta_ref, own_ref, w_out, do_out,
):
    own_ref[...] = mixed_ref[:, lanes(place_ref[0] * own_ref.shape[1], own_ref.shape[1])]
    w_out[...] = w_ref[...]
    do_out[...] = do_ref[...]
    heads, tokens = decay_ref.shape
    row, col = iotas(tokens, tokens)
    cum = prefix_sums(decay_ref[...])
    beta = sigmoid(logit_ref[...])
    beta_ref[...] = beta
    cols = jnp.concatenate([cum, beta], axis=0).T
    for g in range(heads // RATIO):
        first = g * RATIO
        for h in range(first, first + RATIO):
            ratio = jnp.exp(jnp.minimum(cols[:, h : h + 1] - cum[h : h + 1], 0.0))
            causal_ref[h] = jnp.where(col <= row, ratio, 0.0)
        cum_c = cols[:, first : first + RATIO]
        gates_ref[g, :, :RATIO] = cols[:, heads + first : heads + first + RATIO]
        gates_ref[g, :, RATIO : 2 * RATIO] = jnp.exp(cum_c)
        gates_ref[g, :, 2 * RATIO : 3 * RATIO] = jnp.exp(cum_c[tokens - 1 :] - cum_c)


def wide_gates(gates_ref, group, h):
    tokens = gates_ref.shape[1]
    cols = [gates_ref[group, :, i * RATIO + h : i * RATIO + h + 1] for i in range(3)]
    return [jnp.broadcast_to(c, (tokens, DK)) for c in cols]


def group_at(place_ref, slot):
    first, flip = slot
    return first if flip is None else first + ((place_ref[1] & 1) ^ flip)


def lanes(start, size):
    return pl.ds(start if isinstance(start, int) else pl.multiple_of(start, size), size)


def local_kernel(slots, place_ref, *refs):
    each = len(slots)
    outs, exts = (refs[-6 * each : -each], refs[-each:])
    groups = [group_at(place_ref, slot) for slot in slots]
    lowers = []
    for at, group in enumerate(groups):
        lowers += group_system(
            group, place_ref, refs[: -6 * each], *outs[at : 3 * each : each], exts[at]
        )
    inverses = unit_lower_inverses(lowers)
    for at, group in enumerate(groups):
        group_maps(
            group, inverses[at * RATIO : (at + 1) * RATIO], refs[: -6 * each], *outs[each + at :: each]
        )


def group_system(group, place_ref, refs, x_out, act_ref, slope_ref, ext):
    *piece_refs, halo_ref, w_ref, causal_ref, gates_in, do_ref = refs
    mine = place_ref[0]
    here = lanes(group * GROUP, GROUP)
    count = piece_refs[0].shape[0]
    pieces = len(piece_refs)
    tokens = pieces * count
    ext[:EDGE] = halo_ref[:, here].astype(f32)
    x_out[:EDGE] = halo_ref[:, here]
    for s in range(pieces):
        piece = piece_refs[s][:, here]
        begin = pl.multiple_of(EDGE + (mine ^ s) * count, EDGE)
        ext[pl.ds(begin, count)] = piece.astype(f32)
        x_out[pl.ds(begin, count)] = piece
    start = EDGE - (KW - 1)
    conv = w_ref[0:1, here] * ext[start : start + tokens]
    for tap in range(1, KW):
        conv += w_ref[tap : tap + 1, here] * ext[start + tap : start + tap + tokens]
    gate = sigmoid(conv)
    act = conv * gate
    slope = gate + act * (1.0 - gate)
    qn, q_scale = unit_rows(act[:, :DK])
    k, k_scale = unit_rows(act[:, DK : 2 * DK])
    act_ref[:, :DK] = qn
    act_ref[:, DK : 2 * DK] = k
    act_ref[:, 2 * DK :] = act[:, 2 * DK :]
    slope_ref[:, :DK] = slope[:, :DK] * q_scale
    slope_ref[:, DK : 2 * DK] = slope[:, DK : 2 * DK] * k_scale
    slope_ref[:, 2 * DK :] = slope[:, 2 * DK :]
    ks = split(k)
    gram = mm(ks, ks, NT)
    row, col = iotas(tokens, tokens)
    gram = jnp.where(col < row, gram, 0.0)
    lowers = []
    for h in range(RATIO):
        beta = wide_gates(gates_in, group, h)[0]
        wide = jnp.concatenate([beta] * (tokens // DK), axis=1)
        lowers.append(causal_ref[group * RATIO + h] * gram * wide)
    return lowers


def group_maps(group, inverses, refs, act_ref, slope_ref, saved_ref, maps_ref):
    *_, causal_ref, gates_in, do_ref = refs
    tokens = act_ref.shape[0]
    q = act_ref[:, :DK] * DK**-0.5
    k = act_ref[:, DK : 2 * DK]
    scores = mm(split(q), split(k), NT)
    qt = split(q.T)
    kt = split(k.T)
    for h in range(RATIO):
        head = group * RATIO + h
        beta, gamma, tail = wide_gates(gates_in, group, h)
        beta_gamma = beta * gamma
        v = act_ref[:, 2 * DK + h * DV : 2 * DK + (h + 1) * DV]
        do = do_ref[:, lanes(head * DV, DV)]
        solved = mm(split(inverses[h]), split(jnp.concatenate([beta * v, beta_gamma * k], axis=1)))
        du = mm(split((causal_ref[head] * scores).T), (do,))
        pulled = mm(split(inverses[h].T), split(jnp.concatenate([du, tail * k], axis=1)))
        saved_ref[h, :, : DV + DK] = solved
        saved_ref[h, :, DV + DK :] = pulled
        packed = [tail * solved[:, :DV], tail * solved[:, DV:], beta_gamma * pulled[:, :DV]]
        moved = mm(kt, split(jnp.concatenate(packed, axis=1)))
        drow, dcol = iotas(DK, DK)
        total = gamma[tokens - 1 :]
        maps_ref[h, 0] = jnp.where(drow == dcol, total, 0.0) - moved[:, DV : DV + DK]
        maps_ref[h, 1] = moved[:, :DV]
        maps_ref[h, 2] = mm(qt, split(gamma * do.astype(f32))) - moved[:, DV + DK :]


def ordered(core, own, other):
    return (jnp.where(core == 0, own, other), jnp.where(core == 0, other, own))


def compose_kernel(parts, place_ref, *refs):
    keeps, others, outs, held = (refs[:parts], refs[parts : 2 * parts], refs[2 * parts : -1], refs[-1])
    core, chip = (place_ref[1] & 1, place_ref[1] >> 1)
    share = keeps[0].shape[0]
    for p in range(parts):
        for i in range(share):
            maps0, maps1 = ordered(core, keeps[p][i], others[p][i])
            later = mm(split(maps1[0]), split(jnp.concatenate([maps0[0], maps0[1]], axis=1)))
            held[p * share + i, 0] = later[:, :DK]
            held[p * share + i, 1] = later[:, DK:] + maps1[1]
            held[p * share + i, 2] = mm(split(maps0[0].T), split(maps1[2])) + maps0[2]
    for s, out in enumerate(outs):
        out[...] = held[chip ^ s]


def chips_kernel(chips, place_ref, *refs):
    maps_refs, first_ref, last_ref, outs, held, ends = (
        refs[:chips], refs[chips], refs[chips + 1], refs[chips + 2 : -2], refs[-2], refs[-1],
    )
    chip = place_ref[1] >> 1
    for s, maps_ref in enumerate(maps_refs):
        held[chip ^ s] = maps_ref[...]
    share = RATIO
    head = (chip // share * 2 + (place_ref[1] & 1)) * share + chip % share
    state, adjoint = (first_ref[head], last_ref[head])
    for step in range(chips):
        back = chips - 1 - step
        ends[step, 0] = state
        ends[back, 1] = adjoint
        if step < chips - 1:
            state = mm(split(held[step, 0]), split(state)) + held[step, 1]
            adjoint = mm(split(held[back, 0].T), split(adjoint)) + held[back, 2]
    for s, out in enumerate(outs):
        out[...] = ends[chip ^ s]


def expand_kernel(chips, place_ref, *refs):
    ends_refs, refs = (refs[:chips], refs[chips:])
    *maps_refs, own_out, give_out, ends = refs
    parts = len(maps_refs) // 2
    keeps, others = (maps_refs[:parts], maps_refs[parts:])
    core, chip = (place_ref[1] & 1, place_ref[1] >> 1)
    for s, ends_ref in enumerate(ends_refs):
        ends[chip ^ s] = ends_ref[...]
    share = keeps[0].shape[0]
    for p in range(parts):
        for i in range(share):
            head = p * share + i
            state, adjoint = (ends[head, 0], ends[head, 1])
            maps0, maps1 = ordered(core, keeps[p][i], others[p][i])
            state1 = mm(split(maps0[0]), split(state)) + maps0[1]
            adjoint0 = mm(split(maps1[0].T), split(adjoint)) + maps1[2]
            own_out[head, 0], give_out[head, 0] = ordered(core, state, state1)
            own_out[head, 1], give_out[head, 1] = ordered(core, adjoint0, adjoint)


def scan_kernel(maps_ref, first_ref, last_ref, out_ref):
    count = maps_ref.shape[0]
    state, adjoint = (first_ref[0], last_ref[0])
    for step in range(count):
        back = count - 1 - step
        out_ref[step, 0, 0] = state
        out_ref[back, 0, 1] = adjoint
        if step < count - 1:
            state = mm(split(maps_ref[step, 0, 0]), split(state)) + maps_ref[step, 0, 1]
            adjoint = mm(split(maps_ref[back, 0, 0].T), split(adjoint)) + maps_ref[back, 0, 2]


def row_sums(a):
    return dot(jnp.ones((8, 2 * DK), bf16), jnp.concatenate(split(a), axis=1), NT)[:1]


def wide_row_sums(a):
    return dot(jnp.concatenate(split(a), axis=1), jnp.ones((2 * DK, DK), bf16), NN)


def grad_kernel(slots, sides, place_ref, *refs):
    each = len(slots)
    w_ref, beta_ref, causal_ref, gates_in, do_ref, *refs = refs
    ends_refs, refs = (refs[:sides], refs[sides:])
    kept, (*out_refs, dext, ext) = (refs[: 4 * each], refs[4 * each :])
    out_refs, last_refs = (out_refs[:-5], out_refs[-5:])
    for at, slot in enumerate(slots):
        side, first = divmod(at * RATIO, each * RATIO // sides)
        group_grads(
            group_at(place_ref, slot), at, place_ref[0], *kept[4 * at : 4 * at + 4], w_ref, beta_ref,
            causal_ref, gates_in, do_ref, ends_refs[side].at[pl.ds(first, RATIO)], out_refs,
            *last_refs, dext, ext,
        )


def group_grads(
    group, at, mine, x_ref, act_ref, slope_ref, saved_ref, w_ref, beta_ref, causal_ref, gates_in,
    do_ref, ends_ref, out_refs, edge_ref, spill_ref, dw_ref, decay_ref, logit_ref, dext, ext,
):
    tokens = act_ref.shape[0]
    here = lanes(group * GROUP, GROUP)
    there = slice(at * GROUP, (at + 1) * GROUP)
    qn = act_ref[:, :DK]
    q = qn * DK**-0.5
    k = act_ref[:, DK : 2 * DK]
    qs, ks = (split(q), split(k))
    gram = mm(ks, ks, NT)
    scores = mm(qs, ks, NT)
    row, col = iotas(tokens, tokens)
    below = col < row
    suffix = jnp.where(row >= col, 1.0, 0.0).astype(bf16)
    dq, dk = (jnp.zeros((tokens, DK), f32), jnp.zeros((tokens, DK), f32))
    dscores, dgram = (jnp.zeros((tokens, tokens), f32), jnp.zeros((tokens, tokens), f32))
    dvs = []
    for h in range(RATIO):
        head = group * RATIO + h
        beta, gamma, tail = wide_gates(gates_in, group, h)
        v = act_ref[:, 2 * DK + h * DV : 2 * DK + (h + 1) * DV]
        do = (do_ref[:, lanes(head * DV, DV)],)
        state, adjoint = (ends_ref[h, 0], ends_ref[h, 1])
        ss, ds = (split(state), split(adjoint))
        u = saved_ref[h, :, :DV] - mm(split(saved_ref[h, :, DV : DV + DK]), ss)
        z = saved_ref[h, :, DV + DK : 2 * DV + DK] + mm(
            split(saved_ref[h, :, 2 * DV + DK :]), ds
        )
        dv = beta * z
        us, zs = (split(u), split(dv))
        dq_in = gamma * mm(do, ss, NT)
        dk_in = gamma * mm(zs, ss, NT)
        dk_out = tail * mm(us, ds, NT)
        causal = causal_ref[head]
        score_part = mm(do, us, NT) * causal
        gram_part = jnp.where(below, mm(zs, us, NT) * causal, 0.0)
        dscores += score_part
        dgram -= gram_part
        gram_term = gram_part * gram
        both = score_part * scores - gram_term
        dvs.append(dv)
        dq += dq_in
        dk += dk_out - dk_in
        key_in = dk_in * k
        left = dk_out * k
        parts = both[:, :DK]
        terms = gram_term[:, :DK]
        for begin in range(DK, tokens, DK):
            parts += both[:, begin : begin + DK]
            terms += gram_term[:, begin : begin + DK]
        dcum = row_sums(parts + dq_in * q - key_in - left) - jnp.sum(both, axis=0, keepdims=True)
        high, low = split(dcum)
        rest = (dcum - high.astype(f32) - low.astype(f32)).astype(bf16)
        stack = [high, low, rest, high, low, rest, high, low]
        summed = dot(jnp.concatenate(stack, axis=0), suffix, NN)
        at_end = jnp.sum(left, axis=0, keepdims=True) + gamma[tokens - 1 :] * jnp.sum(
            state * adjoint, axis=0, keepdims=True
        )
        decay_ref[pl.ds(head, 1)] = (
            summed[0:1] + summed[1:2] + summed[2:3] + jnp.sum(at_end, axis=1, keepdims=True)
        )
        closed = 1.0 - beta_ref[pl.ds(head, 1)]
        logit_ref[pl.ds(head, 1)] = closed * row_sums(dv * v - terms - key_in)
    dss, dgs = (split(dscores), split(dgram + dgram.T))
    dq += mm(dss, ks)
    dk += mm(split(dscores.T), qs) + mm(dgs, ks)
    dq *= DK**-0.5
    dconv = jnp.concatenate(
        [dq - qn * wide_row_sums(qn * dq), dk - k * wide_row_sums(k * dk)] + dvs, axis=1
    )
    dconv *= slope_ref[...]
    ext[...] = x_ref[...].astype(f32)
    start = EDGE - (KW - 1)
    for tap in range(KW):
        dw_ref[tap : tap + 1, here] = jnp.sum(
            dconv * ext[start + tap : start + tap + tokens], axis=0, keepdims=True
        )
    zero = jnp.zeros((EDGE, GROUP), f32)
    dext[:EDGE] = zero
    dext[EDGE : EDGE + tokens] = dconv
    dext[EDGE + tokens :] = zero
    own = jnp.zeros((tokens, GROUP), f32)
    spill = jnp.zeros((EDGE, GROUP), f32)
    for tap in range(KW):
        begin = EDGE + KW - 1 - tap
        own += w_ref[tap : tap + 1, here] * dext[begin : begin + tokens]
        begin = KW - 1 - tap
        spill += w_ref[tap : tap + 1, here] * dext[begin : begin + EDGE]
    ext[:tokens] = own
    count = tokens // len(out_refs)
    for s, out_ref in enumerate(out_refs):
        begin = pl.multiple_of((mine ^ s) * count, EDGE)
        out_ref[:, there] = ext[pl.ds(begin, count)].astype(bf16)
    edge_ref[:, here] = own[tokens - EDGE :]
    spill_ref[:, here] = spill


def pack_kernel(place_ref, mixed_ref, *outs):
    feats = mixed_ref.shape[1] // (len(outs) + 1)
    for s, out in enumerate(outs):
        out[...] = mixed_ref[:, lanes((place_ref[0] ^ (s + 1)) * feats, feats)]


def assemble_kernel(slots, place_ref, *refs):
    *refs, out_ref = refs
    pieces = len(refs) // 2
    rows = out_ref.shape[0]
    feats = out_ref.shape[1] // pieces
    for at, slot in enumerate(slots):
        for s in range(pieces):
            begin = (place_ref[0] ^ s) * feats + group_at(place_ref, slot) * GROUP
            out_ref[:, lanes(begin, GROUP)] = refs[s][:, at * GROUP : (at + 1) * GROUP]

    @pl.when(place_ref[0] == pieces - 1)
    def fix():
        for s in range(pieces):
            out_ref[rows - EDGE :, s * feats : (s + 1) * feats] = refs[pieces + s][...]


def shape(*dims, dtype=f32):
    return jax.ShapeDtypeStruct(dims, dtype)


def call(kernel, name, out_shape, place, args, scratch=(), flops=0):
    vmem = pl.BlockSpec(memory_space=pltpu.VMEM)
    return pl.pallas_call(
        kernel,
        in_specs=[pl.BlockSpec(memory_space=pltpu.SMEM)] + [vmem] * len(args),
        out_specs=jax.tree.map(lambda _: vmem, out_shape),
        out_shape=out_shape,
        scratch_shapes=scratch,
        compiler_params=pltpu.CompilerParams(vmem_limit_bytes=VMEM_BYTES),
        cost_estimate=pl.CostEstimate(flops=flops, bytes_accessed=1 << 20, transcendentals=0),
        name=name,
    )(place, *args)


def from_behind(value, axis, by):
    devices = lax.axis_size(axis)
    pairs = [(i, i + by) for i in range(devices) if 0 <= i + by < devices]
    return lax.ppermute(value, axis, pairs)


def across(value, axis, by):
    return lax.ppermute(value, axis, [(i, i ^ by) for i in range(lax.axis_size(axis))])


def local_pass(place, slots, received, halo, weight, gates, do):
    tokens = gates[0].shape[1]
    each = len(slots)
    outs = call(
        functools.partial(local_kernel, slots),
        "local_pass",
        [shape(EDGE + tokens, GROUP, dtype=bf16)] * each
        + [shape(tokens, GROUP)] * (2 * each)
        + [shape(RATIO, tokens, 2 * (DV + DK))] * each
        + [shape(RATIO, 3, DK, DV)] * each,
        place,
        [*received, halo, weight, *gates, do],
        [pltpu.VMEM((EDGE + tokens, GROUP), f32)] * each,
        flops=each * 6 * 10**9,
    )
    kept = [outs[at : 4 * each : each] for at in range(each)]
    return (kept, outs[4 * each :])


def grad_pass(place, slots, kept, ends, weight, beta, gates, do, pieces):
    tokens = do.shape[0]
    each = len(slots)
    outs = call(
        functools.partial(grad_kernel, slots, len(ends)),
        "grad_pass",
        [shape(tokens // pieces, each * GROUP, dtype=bf16)] * pieces
        + [
            shape(EDGE, each * GROUP),
            shape(EDGE, each * GROUP),
            shape(KW, each * GROUP),
            shape(each * RATIO, tokens),
            shape(each * RATIO, tokens),
        ],
        place,
        [weight, beta, *gates, do, *ends, *[a for part in kept for a in part]],
        [pltpu.VMEM((tokens + 2 * EDGE, GROUP), f32), pltpu.VMEM((tokens + EDGE, GROUP), f32)],
        flops=each * 4 * 10**9,
    )
    return (outs[:pieces], *outs[pieces:])


def scan_pass(maps, first, last):
    count, heads = maps.shape[:2]
    return pl.pallas_call(
        scan_kernel,
        grid=(heads,),
        in_specs=[
            pl.BlockSpec((count, 1, 3, DK, DV), lambda h: (0, h, 0, 0, 0)),
            pl.BlockSpec((1, DK, DV), lambda h: (h, 0, 0)),
            pl.BlockSpec((1, DK, DV), lambda h: (h, 0, 0)),
        ],
        out_specs=pl.BlockSpec((count, 1, 2, DK, DV), lambda h: (0, h, 0, 0, 0)),
        out_shape=shape(count, heads, 2, DK, DV),
        compiler_params=pltpu.CompilerParams(vmem_limit_bytes=4 * VMEM_BYTES),
        name="scan_pass",
    )(maps, first, last)


def cross_chips(place, keeps, others, initial_state, final_state_grad):
    parts = len(keeps)
    chips = parts * keeps[0].shape[0]
    joined = call(
        functools.partial(compose_kernel, parts),
        "join_cores",
        [shape(3, DK, DV)] * chips,
        place,
        [*keeps, *others],
        [pltpu.VMEM((chips, 3, DK, DV), f32)],
    )
    held = [joined[0]] + [across(joined[s], "ctx", 2 * s) for s in range(1, chips)]
    ends = call(
        functools.partial(chips_kernel, chips),
        "over_chips",
        [shape(2, DK, DV)] * chips,
        place,
        [*held, initial_state, final_state_grad],
        [pltpu.VMEM((chips, 3, DK, DV), f32), pltpu.VMEM((chips, 2, DK, DV), f32)],
    )
    ends = [ends[0]] + [across(ends[s], "ctx", 2 * s) for s in range(1, chips)]
    own, give = call(
        functools.partial(expand_kernel, chips),
        "within_chip",
        [shape(chips, 2, DK, DV)] * 2,
        place,
        [*ends, *keeps, *others],
        [pltpu.VMEM((chips, 2, DK, DV), f32)],
    )
    return (own, across(give, "ctx", 1))


def on_device(
    mixed_in,
    conv_weight,
    write_strength_logit,
    decay_log,
    initial_state,
    final_state_grad,
    grad_out,
):
    devices, pieces = (lax.axis_size("ctx"), lax.axis_size("head"))
    heads, tokens = decay_log.shape
    groups = heads // RATIO
    feats = groups * GROUP
    paired = heads == devices and groups == 4
    slots = tuple((g, None) for g in range(groups))
    if paired:
        slots = tuple((g, flip) for flip in (1, 0) for g in range(0, groups, 2))
    place = jnp.stack([lax.axis_index("head"), lax.axis_index("ctx")]).astype(jnp.int32)
    packed = call(
        pack_kernel,
        "pack",
        [shape(mixed_in.shape[0], feats, dtype=bf16)] * (pieces - 1),
        place,
        [mixed_in],
    )
    arrived = [across(piece, "head", s + 1) for s, piece in enumerate(packed)]
    causal, gates, beta, own_piece, near_weight, near_do = call(
        gates_kernel,
        "gates_pass",
        [
            shape(heads, tokens, tokens),
            shape(groups, tokens, 8),
            shape(heads, tokens),
            shape(mixed_in.shape[0], feats, dtype=bf16),
            shape(*conv_weight.shape),
            shape(*grad_out.shape, dtype=bf16),
        ],
        place,
        [write_strength_logit, decay_log, mixed_in, conv_weight, grad_out],
    )
    arrived[0], own_piece = lax.optimization_barrier((arrived[0], own_piece))
    arrived = [own_piece, *arrived]
    gates = (causal, gates)
    mine = lax.axis_index("head")
    edge_rows = own_piece[own_piece.shape[0] - EDGE :]
    for s in range(1, pieces):
        edge_rows = jnp.where((mine ^ s) == pieces - 1, arrived[s][-EDGE:], edge_rows)
    halo = from_behind(edge_rows, "ctx", 1)
    kept, maps = local_pass(place, slots, arrived, halo, near_weight, gates, near_do)
    if paired:
        others = [across(part, "ctx", 1) for part in maps[: groups // 2]]
        own_ends, other_ends = cross_chips(
            place, maps[groups // 2 :], others, initial_state, final_state_grad
        )
        ends = [other_ends, own_ends]
    else:
        gathered = lax.all_gather(jnp.concatenate(maps), "ctx")
        gathered = scan_pass(gathered, initial_state, final_state_grad)
        ends = [lax.dynamic_index_in_dim(gathered, lax.axis_index("ctx"), 0, keepdims=False)]
    out_pieces, edge, spill, dweight, grad_decay, grad_beta = grad_pass(
        place, slots, kept, ends, conv_weight, beta, gates, grad_out, pieces
    )
    received = [out_pieces[0]] + [across(out_pieces[s], "head", s) for s in range(1, pieces)]
    last = (edge + from_behind(spill, "ctx", -1)).astype(bf16)
    last_rows = [
        lax.ppermute(
            last, ("ctx", "head"), [(c * pieces + h, (c + 1) * pieces - 1) for c in range(devices)]
        )
        for h in range(pieces - 1)
    ] + [last]
    returned = call(
        functools.partial(assemble_kernel, slots),
        "assemble",
        shape(mixed_in.shape[0], feats * pieces, dtype=bf16),
        place,
        [*received, *last_rows],
    )
    if devices & (devices - 1) == 0:
        by = 1
        while by < devices:
            dweight = dweight + across(dweight, "ctx", by)
            by *= 2
    else:
        dweight = lax.psum(dweight, "ctx")
    return (returned, dweight, grad_beta, grad_decay)


def solution(mesh):
    in_specs = (
        P(("ctx", "head"), None),
        P(None, "head"),
        P("head", "ctx"),
        P("head", "ctx"),
        P("head", None, None),
        P("head", None, None),
        P("ctx", "head"),
    )
    out_specs = (P(("ctx", "head"), None), P(None, "head"), P("head", "ctx"), P("head", "ctx"))
    return jax.shard_map(
        on_device, mesh=mesh, in_specs=in_specs, out_specs=out_specs, check_vma=False
    )
```

```python
import functools
import jax
import jax.numpy as jnp
from jax import lax
from jax.experimental import pallas as pl
from jax.experimental.pallas import tpu as pltpu
from jax.sharding import PartitionSpec as P

HK = 16
VALUE_HEADS = 32
DK = 128
DV = 128
KW = 4
RATIO = VALUE_HEADS // HK
GROUP = 2 * DK + RATIO * DV
TILE = 128
BASE = 2
STEP = 2
EDGE = 16
VMEM_BYTES = 24 * 1024 * 1024

norm_eps = 1e-06
f32 = jnp.float32
bf16 = jnp.bfloat16
NN = (((1,), (0,)), ((), ()))
NT = (((1,), (1,)), ((), ()))


def split(a):
    high = a.astype(bf16)
    return (high, (a - high.astype(f32)).astype(bf16))


def dot(a, b, dims):
    return lax.dot_general(a, b, dims, preferred_element_type=f32)


def mm(a, b, dims=NN):
    inner_axis = dims[0][1][0]
    inner, outer = (b[0].shape[inner_axis], b[0].shape[1 - inner_axis])
    if len(b) == 1:
        return dot(a[0], b[0], dims) + dot(a[1], b[0], dims)
    high, low = b
    exact = len(a) == 1
    if outer <= TILE:
        wide = jnp.concatenate([high, low], axis=1 - inner_axis)
        if exact:
            total = dot(a[0], wide, dims)
        elif inner <= TILE:
            both = jnp.concatenate([wide, wide], axis=inner_axis)
            total = dot(jnp.concatenate(a, axis=1), both, dims)
        else:
            total = dot(a[0], wide, dims) + dot(a[1], wide, dims)
        return total[:, :outer] + total[:, outer:]
    if inner <= TILE:
        if exact:
            deep = jnp.concatenate([high, low], axis=inner_axis)
            return dot(jnp.concatenate([a[0], a[0]], axis=1), deep, dims)
        deep = jnp.concatenate([high, high], axis=inner_axis)
        return dot(jnp.concatenate(a, axis=1), deep, dims) + dot(a[0], low, dims)
    total = dot(a[0], high, dims) + dot(a[0], low, dims)
    return total if exact else total + dot(a[1], high, dims)


def together(works):
    works = list(works)
    while works:
        works = [work for work in works if next(work, works) is None]
        yield


def finish(work):
    for _ in work:
        pass


def iotas(rows, cols):
    return (
        lax.broadcasted_iota(jnp.int32, (rows, cols), 0),
        lax.broadcasted_iota(jnp.int32, (rows, cols), 1),
    )


def tile_inverses(lowers):
    row, col = iotas(TILE, TILE)
    eye = jnp.where(row == col, 1.0, 0.0).astype(f32)
    width = BASE
    same = row // width == col // width
    inverses = [eye - jnp.where(same, low, 0.0) for low in lowers]
    while width < TILE:
        same = row // width == col // width
        wider = row // (2 * width) == col // (2 * width)
        between = wider & jnp.logical_not(same)
        parts = [split(inv) for inv in inverses]
        inner = [
            mm(split(jnp.where(between, low, 0.0)), inv) for low, inv in zip(lowers, parts)
        ]
        inverses = [inv - mm(p, split(i)) for inv, p, i in zip(inverses, parts, inner)]
        width *= 2
    return inverses


def unit_lower_inverses(lowers):
    size = lowers[0].shape[0]
    if size == TILE:
        return tile_inverses(lowers)
    half = size // 2
    inverses = unit_lower_inverses(
        [low[:half, :half] for low in lowers] + [low[half:, half:] for low in lowers]
    )
    first, second = (inverses[: len(lowers)], inverses[len(lowers) :])
    inner = [mm(split(low[half:, :half]), split(inv)) for low, inv in zip(lowers, first)]
    below = [-mm(split(inv), split(i)) for inv, i in zip(second, inner)]
    zero = jnp.zeros((half, half), f32)
    return [
        jnp.concatenate(
            [jnp.concatenate([a, zero], axis=1), jnp.concatenate([c, b], axis=1)], axis=0
        )
        for a, b, c in zip(first, second, below)
    ]


def sigmoid(a):
    return 1.0 / (1.0 + jnp.exp(-a))


def unit_rows(a):
    scale = lax.rsqrt(jnp.sum(a * a, axis=-1, keepdims=True) + norm_eps)
    return (a * scale, scale)


def prefix_sums(a):
    count, size = a.shape
    high, low = split(a)
    rest = (a - high.astype(f32) - low.astype(f32)).astype(bf16)
    row, col = iotas(size, size)
    parts = dot(
        jnp.concatenate([high, low, rest], axis=0), jnp.where(row <= col, 1.0, 0.0).astype(bf16), NN
    )
    return parts[:count] + parts[count : 2 * count] + parts[2 * count :]


def gates_kernel(
    place_ref, logit_ref, decay_ref, mixed_ref, w_ref, do_ref,
    causal_ref, gates_ref, beta_ref, own_ref, w_out, do_out,
):
    own_ref[...] = mixed_ref[:, lanes(place_ref[0] * own_ref.shape[1], own_ref.shape[1])]
    w_out[...] = w_ref[...]
    do_out[...] = do_ref[...]
    heads, tokens = decay_ref.shape
    row, col = iotas(tokens, tokens)
    cum = prefix_sums(decay_ref[...])
    beta = sigmoid(logit_ref[...])
    beta_ref[...] = beta
    cols = jnp.concatenate([cum, beta], axis=0).T
    for g in range(heads // RATIO):
        first = g * RATIO
        for h in range(first, first + RATIO):
            ratio = jnp.exp(jnp.minimum(cols[:, h : h + 1] - cum[h : h + 1], 0.0))
            causal_ref[h] = jnp.where(col <= row, ratio, 0.0)
        cum_c = cols[:, first : first + RATIO]
        gates_ref[g, :, :RATIO] = cols[:, heads + first : heads + first + RATIO]
        gates_ref[g, :, RATIO : 2 * RATIO] = jnp.exp(cum_c)
        gates_ref[g, :, 2 * RATIO : 3 * RATIO] = jnp.exp(cum_c[tokens - 1 :] - cum_c)


def wide_gates(gates_ref, group, h):
    tokens = gates_ref.shape[1]
    cols = [gates_ref[group, :, i * RATIO + h : i * RATIO + h + 1] for i in range(3)]
    return [jnp.broadcast_to(c, (tokens, DK)) for c in cols]


def group_at(place_ref, slot):
    first, flip = slot
    return first if flip is None else first + ((place_ref[1] & 1) ^ flip)


def lanes(start, size):
    return pl.ds(start if isinstance(start, int) else pl.multiple_of(start, size), size)


def local_kernel(slots, place_ref, *refs):
    each = len(slots)
    outs, exts = (refs[-6 * each : -each], refs[-each:])
    groups = [group_at(place_ref, slot) for slot in slots]
    lowers = []
    for at, group in enumerate(groups):
        lowers += group_system(
            group, place_ref, refs[: -6 * each], *outs[at : 3 * each : each], exts[at]
        )
    inverses = unit_lower_inverses(lowers)
    for at, group in enumerate(groups):
        finish(
            group_maps(
                group, inverses[at * RATIO : (at + 1) * RATIO], refs[: -6 * each],
                *outs[each + at :: each],
            )
        )


def group_system(group, place_ref, refs, x_out, act_ref, slope_ref, ext):
    *piece_refs, halo_ref, w_ref, causal_ref, gates_in, do_ref = refs
    mine = place_ref[0]
    here = lanes(group * GROUP, GROUP)
    count = piece_refs[0].shape[0]
    pieces = len(piece_refs)
    tokens = pieces * count
    ext[:EDGE] = halo_ref[:, here].astype(f32)
    x_out[:EDGE] = halo_ref[:, here]
    for s in range(pieces):
        piece = piece_refs[s][:, here]
        begin = pl.multiple_of(EDGE + (mine ^ s) * count, EDGE)
        ext[pl.ds(begin, count)] = piece.astype(f32)
        x_out[pl.ds(begin, count)] = piece
    start = EDGE - (KW - 1)
    conv = w_ref[0:1, here] * ext[start : start + tokens]
    for tap in range(1, KW):
        conv += w_ref[tap : tap + 1, here] * ext[start + tap : start + tap + tokens]
    gate = sigmoid(conv)
    act = conv * gate
    slope = gate + act * (1.0 - gate)
    qn, q_scale = unit_rows(act[:, :DK])
    k, k_scale = unit_rows(act[:, DK : 2 * DK])
    act_ref[:, :DK] = qn
    act_ref[:, DK : 2 * DK] = k
    act_ref[:, 2 * DK :] = act[:, 2 * DK :]
    slope_ref[:, :DK] = slope[:, :DK] * q_scale
    slope_ref[:, DK : 2 * DK] = slope[:, DK : 2 * DK] * k_scale
    slope_ref[:, 2 * DK :] = slope[:, 2 * DK :]
    ks = split(k)
    gram = mm(ks, ks, NT)
    row, col = iotas(tokens, tokens)
    gram = jnp.where(col < row, gram, 0.0)
    lowers = []
    for h in range(RATIO):
        beta = wide_gates(gates_in, group, h)[0]
        wide = jnp.concatenate([beta] * (tokens // DK), axis=1)
        lowers.append(causal_ref[group * RATIO + h] * gram * wide)
    return lowers


def group_maps(group, inverses, refs, act_ref, slope_ref, saved_ref, maps_ref):
    *_, causal_ref, gates_in, do_ref = refs
    tokens = act_ref.shape[0]
    q = act_ref[:, :DK] * DK**-0.5
    k = act_ref[:, DK : 2 * DK]
    scores = mm(split(q), split(k), NT)
    qt = split(q.T)
    kt = split(k.T)
    yield

    def head_maps(h):
        head = group * RATIO + h
        beta, gamma, tail = wide_gates(gates_in, group, h)
        beta_gamma = beta * gamma
        v = act_ref[:, 2 * DK + h * DV : 2 * DK + (h + 1) * DV]
        do = do_ref[:, lanes(head * DV, DV)]
        solved = mm(split(inverses[h]), split(jnp.concatenate([beta * v, beta_gamma * k], axis=1)))
        du = mm(split((causal_ref[head] * scores).T), (do,))
        yield
        saved_ref[h, :, : DV + DK] = solved
        pulled = mm(split(inverses[h].T), split(jnp.concatenate([du, tail * k], axis=1)))
        yield
        saved_ref[h, :, DV + DK :] = pulled
        packed = [tail * solved[:, :DV], tail * solved[:, DV:], beta_gamma * pulled[:, :DV]]
        moved = mm(kt, split(jnp.concatenate(packed, axis=1)))
        adjoint = mm(qt, split(gamma * do.astype(f32)))
        yield
        drow, dcol = iotas(DK, DK)
        total = gamma[tokens - 1 :]
        maps_ref[h, 0] = jnp.where(drow == dcol, total, 0.0) - moved[:, DV : DV + DK]
        maps_ref[h, 1] = moved[:, :DV]
        maps_ref[h, 2] = adjoint - moved[:, DV + DK :]

    yield from together(head_maps(h) for h in range(RATIO))


def ordered(core, own, other):
    return (jnp.where(core == 0, own, other), jnp.where(core == 0, other, own))


def compose_kernel(parts, place_ref, *refs):
    keeps, others, outs, held = (refs[:parts], refs[parts : 2 * parts], refs[2 * parts : -1], refs[-1])
    core, chip = (place_ref[1] & 1, place_ref[1] >> 1)
    share = keeps[0].shape[0]
    for p in range(parts):
        for i in range(share):
            maps0, maps1 = ordered(core, keeps[p][i], others[p][i])
            later = mm(split(maps1[0]), split(jnp.concatenate([maps0[0], maps0[1]], axis=1)))
            held[p * share + i, 0] = later[:, :DK]
            held[p * share + i, 1] = later[:, DK:] + maps1[1]
            held[p * share + i, 2] = mm(split(maps0[0].T), split(maps1[2])) + maps0[2]
    for s, out in enumerate(outs):
        out[...] = held[chip ^ s]


def chips_kernel(chips, place_ref, *refs):
    maps_refs, first_ref, last_ref, outs, held, ends = (
        refs[:chips], refs[chips], refs[chips + 1], refs[chips + 2 : -2], refs[-2], refs[-1],
    )
    chip = place_ref[1] >> 1
    for s, maps_ref in enumerate(maps_refs):
        held[chip ^ s] = maps_ref[...]
    share = RATIO
    head = (chip // share * 2 + (place_ref[1] & 1)) * share + chip % share
    state, adjoint = (first_ref[head], last_ref[head])
    for step in range(chips):
        back = chips - 1 - step
        ends[step, 0] = state
        ends[back, 1] = adjoint
        if step < chips - 1:
            state = mm(split(held[step, 0]), split(state)) + held[step, 1]
            adjoint = mm(split(held[back, 0].T), split(adjoint)) + held[back, 2]
    for s, out in enumerate(outs):
        out[...] = ends[chip ^ s]


def expand_kernel(chips, place_ref, *refs):
    ends_refs, refs = (refs[:chips], refs[chips:])
    *maps_refs, own_out, give_out, ends = refs
    parts = len(maps_refs) // 2
    keeps, others = (maps_refs[:parts], maps_refs[parts:])
    core, chip = (place_ref[1] & 1, place_ref[1] >> 1)
    for s, ends_ref in enumerate(ends_refs):
        ends[chip ^ s] = ends_ref[...]
    share = keeps[0].shape[0]
    for p in range(parts):
        for i in range(share):
            head = p * share + i
            state, adjoint = (ends[head, 0], ends[head, 1])
            maps0, maps1 = ordered(core, keeps[p][i], others[p][i])
            state1 = mm(split(maps0[0]), split(state)) + maps0[1]
            adjoint0 = mm(split(maps1[0].T), split(adjoint)) + maps1[2]
            own_out[head, 0], give_out[head, 0] = ordered(core, state, state1)
            own_out[head, 1], give_out[head, 1] = ordered(core, adjoint0, adjoint)


def scan_kernel(maps_ref, first_ref, last_ref, out_ref):
    count = maps_ref.shape[0]
    state, adjoint = (first_ref[0], last_ref[0])
    for step in range(count):
        back = count - 1 - step
        out_ref[step, 0, 0] = state
        out_ref[back, 0, 1] = adjoint
        if step < count - 1:
            state = mm(split(maps_ref[step, 0, 0]), split(state)) + maps_ref[step, 0, 1]
            adjoint = mm(split(maps_ref[back, 0, 0].T), split(adjoint)) + maps_ref[back, 0, 2]


def row_sums(a):
    return dot(jnp.ones((8, 2 * DK), bf16), jnp.concatenate(split(a), axis=1), NT)[:1]


def wide_row_sums(a):
    return dot(jnp.concatenate(split(a), axis=1), jnp.ones((2 * DK, DK), bf16), NN)


def grad_kernel(slots, sides, place_ref, *refs):
    each = len(slots)
    w_ref, beta_ref, causal_ref, gates_in, do_ref, *refs = refs
    ends_refs, refs = (refs[:sides], refs[sides:])
    kept, (*out_refs, dext, ext) = (refs[: 4 * each], refs[4 * each :])
    out_refs, last_refs = (out_refs[:-5], out_refs[-5:])
    works = []
    for at, slot in enumerate(slots):
        side, first = divmod(at * RATIO, each * RATIO // sides)
        works.append(
            group_grads(
                group_at(place_ref, slot), at, place_ref[0], *kept[4 * at : 4 * at + 4], w_ref,
                beta_ref, causal_ref, gates_in, do_ref, ends_refs[side].at[pl.ds(first, RATIO)],
                out_refs, *last_refs, dext.at[at % STEP], ext.at[at % STEP],
            )
        )
    for first in range(0, each, STEP):
        finish(together(works[first : first + STEP]))


def group_grads(
    group, at, mine, x_ref, act_ref, slope_ref, saved_ref, w_ref, beta_ref, causal_ref, gates_in,
    do_ref, ends_ref, out_refs, edge_ref, spill_ref, dw_ref, decay_ref, logit_ref, dext, ext,
):
    tokens = act_ref.shape[0]
    here = lanes(group * GROUP, GROUP)
    there = slice(at * GROUP, (at + 1) * GROUP)
    qn = act_ref[:, :DK]
    q = qn * DK**-0.5
    k = act_ref[:, DK : 2 * DK]
    qs, ks = (split(q), split(k))
    gram = mm(ks, ks, NT)
    scores = mm(qs, ks, NT)
    row, col = iotas(tokens, tokens)
    below = col < row
    suffix = jnp.where(row >= col, 1.0, 0.0).astype(bf16)
    yield
    results = [None] * RATIO

    def head_grads(h):
        head = group * RATIO + h
        beta, gamma, tail = wide_gates(gates_in, group, h)
        v = act_ref[:, 2 * DK + h * DV : 2 * DK + (h + 1) * DV]
        do = (do_ref[:, lanes(head * DV, DV)],)
        state, adjoint = (ends_ref[h, 0], ends_ref[h, 1])
        ss, ds = (split(state), split(adjoint))
        u = saved_ref[h, :, :DV] - mm(split(saved_ref[h, :, DV : DV + DK]), ss)
        z = saved_ref[h, :, DV + DK : 2 * DV + DK] + mm(
            split(saved_ref[h, :, 2 * DV + DK :]), ds
        )
        yield
        dv = beta * z
        us, zs = (split(u), split(dv))
        dq_in = gamma * mm(do, ss, NT)
        dk_in = gamma * mm(zs, ss, NT)
        dk_out = tail * mm(us, ds, NT)
        yield
        causal = causal_ref[head]
        score_part = mm(do, us, NT) * causal
        gram_part = jnp.where(below, mm(zs, us, NT) * causal, 0.0)
        yield
        gram_term = gram_part * gram
        both = score_part * scores - gram_term
        key_in = dk_in * k
        left = dk_out * k
        parts = both[:, :DK]
        terms = gram_term[:, :DK]
        for begin in range(DK, tokens, DK):
            parts += both[:, begin : begin + DK]
            terms += gram_term[:, begin : begin + DK]
        dcum = row_sums(parts + dq_in * q - key_in - left) - jnp.sum(both, axis=0, keepdims=True)
        results[h] = (dq_in, dk_out - dk_in, dv, score_part, gram_part)
        yield
        high, low = split(dcum)
        rest = (dcum - high.astype(f32) - low.astype(f32)).astype(bf16)
        stack = [high, low, rest, high, low, rest, high, low]
        summed = dot(jnp.concatenate(stack, axis=0), suffix, NN)
        at_end = jnp.sum(left, axis=0, keepdims=True) + gamma[tokens - 1 :] * jnp.sum(
            state * adjoint, axis=0, keepdims=True
        )
        decay_ref[pl.ds(head, 1)] = (
            summed[0:1] + summed[1:2] + summed[2:3] + jnp.sum(at_end, axis=1, keepdims=True)
        )
        closed = 1.0 - beta_ref[pl.ds(head, 1)]
        logit_ref[pl.ds(head, 1)] = closed * row_sums(dv * v - terms - key_in)

    yield from together(head_grads(h) for h in range(RATIO))
    dq, dk, _, dscores, dgram = (sum(parts[1:], parts[0]) for parts in zip(*results))
    dgram = -dgram
    dvs = [result[2] for result in results]
    dss, dgs = (split(dscores), split(dgram + dgram.T))
    dq += mm(dss, ks)
    dk += mm(split(dscores.T), qs) + mm(dgs, ks)
    yield
    dq *= DK**-0.5
    dconv = jnp.concatenate(
        [dq - qn * wide_row_sums(qn * dq), dk - k * wide_row_sums(k * dk)] + dvs, axis=1
    )
    dconv *= slope_ref[...]
    ext[...] = x_ref[...].astype(f32)
    start = EDGE - (KW - 1)
    for tap in range(KW):
        dw_ref[tap : tap + 1, here] = jnp.sum(
            dconv * ext[start + tap : start + tap + tokens], axis=0, keepdims=True
        )
    zero = jnp.zeros((EDGE, GROUP), f32)
    yield
    dext[:EDGE] = zero
    dext[EDGE : EDGE + tokens] = dconv
    dext[EDGE + tokens :] = zero
    own = jnp.zeros((tokens, GROUP), f32)
    spill = jnp.zeros((EDGE, GROUP), f32)
    for tap in range(KW):
        begin = EDGE + KW - 1 - tap
        own += w_ref[tap : tap + 1, here] * dext[begin : begin + tokens]
        begin = KW - 1 - tap
        spill += w_ref[tap : tap + 1, here] * dext[begin : begin + EDGE]
    ext[:tokens] = own
    count = tokens // len(out_refs)
    for s, out_ref in enumerate(out_refs):
        begin = pl.multiple_of((mine ^ s) * count, EDGE)
        out_ref[:, there] = ext[pl.ds(begin, count)].astype(bf16)
    edge_ref[:, here] = own[tokens - EDGE :]
    spill_ref[:, here] = spill


def pack_kernel(place_ref, mixed_ref, *outs):
    feats = mixed_ref.shape[1] // (len(outs) + 1)
    for s, out in enumerate(outs):
        out[...] = mixed_ref[:, lanes((place_ref[0] ^ (s + 1)) * feats, feats)]


def assemble_kernel(slots, place_ref, *refs):
    *refs, out_ref = refs
    pieces = len(refs) // 2
    rows = out_ref.shape[0]
    feats = out_ref.shape[1] // pieces
    for at, slot in enumerate(slots):
        for s in range(pieces):
            begin = (place_ref[0] ^ s) * feats + group_at(place_ref, slot) * GROUP
            out_ref[:, lanes(begin, GROUP)] = refs[s][:, at * GROUP : (at + 1) * GROUP]

    @pl.when(place_ref[0] == pieces - 1)
    def fix():
        for s in range(pieces):
            out_ref[rows - EDGE :, s * feats : (s + 1) * feats] = refs[pieces + s][...]


def shape(*dims, dtype=f32):
    return jax.ShapeDtypeStruct(dims, dtype)


def call(kernel, name, out_shape, place, args, scratch=(), flops=0):
    vmem = pl.BlockSpec(memory_space=pltpu.VMEM)
    return pl.pallas_call(
        kernel,
        in_specs=[pl.BlockSpec(memory_space=pltpu.SMEM)] + [vmem] * len(args),
        out_specs=jax.tree.map(lambda _: vmem, out_shape),
        out_shape=out_shape,
        scratch_shapes=scratch,
        compiler_params=pltpu.CompilerParams(vmem_limit_bytes=VMEM_BYTES),
        cost_estimate=pl.CostEstimate(flops=flops, bytes_accessed=1 << 20, transcendentals=0),
        name=name,
    )(place, *args)


def from_behind(value, axis, by):
    devices = lax.axis_size(axis)
    pairs = [(i, i + by) for i in range(devices) if 0 <= i + by < devices]
    return lax.ppermute(value, axis, pairs)


def across(value, axis, by):
    return lax.ppermute(value, axis, [(i, i ^ by) for i in range(lax.axis_size(axis))])


def local_pass(place, slots, received, halo, weight, gates, do):
    tokens = gates[0].shape[1]
    each = len(slots)
    outs = call(
        functools.partial(local_kernel, slots),
        "local_pass",
        [shape(EDGE + tokens, GROUP, dtype=bf16)] * each
        + [shape(tokens, GROUP)] * (2 * each)
        + [shape(RATIO, tokens, 2 * (DV + DK))] * each
        + [shape(RATIO, 3, DK, DV)] * each,
        place,
        [*received, halo, weight, *gates, do],
        [pltpu.VMEM((EDGE + tokens, GROUP), f32)] * each,
        flops=each * 6 * 10**9,
    )
    kept = [outs[at : 4 * each : each] for at in range(each)]
    return (kept, outs[4 * each :])


def grad_pass(place, slots, kept, ends, weight, beta, gates, do, pieces):
    tokens = do.shape[0]
    each = len(slots)
    outs = call(
        functools.partial(grad_kernel, slots, len(ends)),
        "grad_pass",
        [shape(tokens // pieces, each * GROUP, dtype=bf16)] * pieces
        + [
            shape(EDGE, each * GROUP),
            shape(EDGE, each * GROUP),
            shape(KW, each * GROUP),
            shape(each * RATIO, tokens),
            shape(each * RATIO, tokens),
        ],
        place,
        [weight, beta, *gates, do, *ends, *[a for part in kept for a in part]],
        [
            pltpu.VMEM((STEP, tokens + 2 * EDGE, GROUP), f32),
            pltpu.VMEM((STEP, tokens + EDGE, GROUP), f32),
        ],
        flops=each * 4 * 10**9,
    )
    return (outs[:pieces], *outs[pieces:])


def scan_pass(maps, first, last):
    count, heads = maps.shape[:2]
    return pl.pallas_call(
        scan_kernel,
        grid=(heads,),
        in_specs=[
            pl.BlockSpec((count, 1, 3, DK, DV), lambda h: (0, h, 0, 0, 0)),
            pl.BlockSpec((1, DK, DV), lambda h: (h, 0, 0)),
            pl.BlockSpec((1, DK, DV), lambda h: (h, 0, 0)),
        ],
        out_specs=pl.BlockSpec((count, 1, 2, DK, DV), lambda h: (0, h, 0, 0, 0)),
        out_shape=shape(count, heads, 2, DK, DV),
        compiler_params=pltpu.CompilerParams(vmem_limit_bytes=4 * VMEM_BYTES),
        name="scan_pass",
    )(maps, first, last)


def cross_chips(place, keeps, others, initial_state, final_state_grad):
    parts = len(keeps)
    chips = parts * keeps[0].shape[0]
    joined = call(
        functools.partial(compose_kernel, parts),
        "join_cores",
        [shape(3, DK, DV)] * chips,
        place,
        [*keeps, *others],
        [pltpu.VMEM((chips, 3, DK, DV), f32)],
    )
    held = [joined[0]] + [across(joined[s], "ctx", 2 * s) for s in range(1, chips)]
    ends = call(
        functools.partial(chips_kernel, chips),
        "over_chips",
        [shape(2, DK, DV)] * chips,
        place,
        [*held, initial_state, final_state_grad],
        [pltpu.VMEM((chips, 3, DK, DV), f32), pltpu.VMEM((chips, 2, DK, DV), f32)],
    )
    ends = [ends[0]] + [across(ends[s], "ctx", 2 * s) for s in range(1, chips)]
    own, give = call(
        functools.partial(expand_kernel, chips),
        "within_chip",
        [shape(chips, 2, DK, DV)] * 2,
        place,
        [*ends, *keeps, *others],
        [pltpu.VMEM((chips, 2, DK, DV), f32)],
    )
    return (own, across(give, "ctx", 1))


def on_device(
    mixed_in,
    conv_weight,
    write_strength_logit,
    decay_log,
    initial_state,
    final_state_grad,
    grad_out,
):
    devices, pieces = (lax.axis_size("ctx"), lax.axis_size("head"))
    heads, tokens = decay_log.shape
    groups = heads // RATIO
    feats = groups * GROUP
    paired = heads == devices and groups == 4
    slots = tuple((g, None) for g in range(groups))
    if paired:
        slots = tuple((g, flip) for flip in (1, 0) for g in range(0, groups, 2))
    place = jnp.stack([lax.axis_index("head"), lax.axis_index("ctx")]).astype(jnp.int32)
    packed = call(
        pack_kernel,
        "pack",
        [shape(mixed_in.shape[0], feats, dtype=bf16)] * (pieces - 1),
        place,
        [mixed_in],
    )
    arrived = [across(piece, "head", s + 1) for s, piece in enumerate(packed)]
    causal, gates, beta, own_piece, near_weight, near_do = call(
        gates_kernel,
        "gates_pass",
        [
            shape(heads, tokens, tokens),
            shape(groups, tokens, 8),
            shape(heads, tokens),
            shape(mixed_in.shape[0], feats, dtype=bf16),
            shape(*conv_weight.shape),
            shape(*grad_out.shape, dtype=bf16),
        ],
        place,
        [write_strength_logit, decay_log, mixed_in, conv_weight, grad_out],
    )
    arrived[0], own_piece = lax.optimization_barrier((arrived[0], own_piece))
    arrived = [own_piece, *arrived]
    gates = (causal, gates)
    mine = lax.axis_index("head")
    edge_rows = own_piece[own_piece.shape[0] - EDGE :]
    for s in range(1, pieces):
        edge_rows = jnp.where((mine ^ s) == pieces - 1, arrived[s][-EDGE:], edge_rows)
    halo = from_behind(edge_rows, "ctx", 1)
    kept, maps = local_pass(place, slots, arrived, halo, near_weight, gates, near_do)
    if paired:
        others = [across(part, "ctx", 1) for part in maps[: groups // 2]]
        own_ends, other_ends = cross_chips(
            place, maps[groups // 2 :], others, initial_state, final_state_grad
        )
        ends = [other_ends, own_ends]
    else:
        gathered = lax.all_gather(jnp.concatenate(maps), "ctx")
        gathered = scan_pass(gathered, initial_state, final_state_grad)
        ends = [lax.dynamic_index_in_dim(gathered, lax.axis_index("ctx"), 0, keepdims=False)]
    out_pieces, edge, spill, dweight, grad_decay, grad_beta = grad_pass(
        place, slots, kept, ends, conv_weight, beta, gates, grad_out, pieces
    )
    received = [out_pieces[0]] + [across(out_pieces[s], "head", s) for s in range(1, pieces)]
    last = (edge + from_behind(spill, "ctx", -1)).astype(bf16)
    last_rows = [
        lax.ppermute(
            last, ("ctx", "head"), [(c * pieces + h, (c + 1) * pieces - 1) for c in range(devices)]
        )
        for h in range(pieces - 1)
    ] + [last]
    returned = call(
        functools.partial(assemble_kernel, slots),
        "assemble",
        shape(mixed_in.shape[0], feats * pieces, dtype=bf16),
        place,
        [*received, *last_rows],
    )
    if devices & (devices - 1) == 0:
        by = 1
        while by < devices:
            dweight = dweight + across(dweight, "ctx", by)
            by *= 2
    else:
        dweight = lax.psum(dweight, "ctx")
    return (returned, dweight, grad_beta, grad_decay)


def solution(mesh):
    in_specs = (
        P(("ctx", "head"), None),
        P(None, "head"),
        P("head", "ctx"),
        P("head", "ctx"),
        P("head", None, None),
        P("head", None, None),
        P("ctx", "head"),
    )
    out_specs = (P(("ctx", "head"), None), P(None, "head"), P("head", "ctx"), P("head", "ctx"))
    return jax.shard_map(
        on_device, mesh=mesh, in_specs=in_specs, out_specs=out_specs, check_vma=False
    )
```

```python
import functools
import jax
import jax.numpy as jnp
from jax import lax
from jax.experimental import pallas as pl
from jax.experimental.pallas import tpu as pltpu
from jax.sharding import PartitionSpec as P

HK = 16
VALUE_HEADS = 32
DK = 128
DV = 128
KW = 4
RATIO = VALUE_HEADS // HK
GROUP = 2 * DK + RATIO * DV
TILE = 128
BASE = 2
STEP = 2
EDGE = 16
VMEM_BYTES = 24 * 1024 * 1024

norm_eps = 1e-06
f32 = jnp.float32
bf16 = jnp.bfloat16
NN = (((1,), (0,)), ((), ()))
NT = (((1,), (1,)), ((), ()))


def split(a):
    high = a.astype(bf16)
    return (high, (a - high.astype(f32)).astype(bf16))


def dot(a, b, dims):
    return lax.dot_general(a, b, dims, preferred_element_type=f32)


def mm(a, b, dims=NN):
    inner_axis = dims[0][1][0]
    inner, outer = (b[0].shape[inner_axis], b[0].shape[1 - inner_axis])
    if len(b) == 1:
        return dot(a[0], b[0], dims) + dot(a[1], b[0], dims)
    high, low = b
    exact = len(a) == 1
    if outer <= TILE:
        wide = jnp.concatenate([high, low], axis=1 - inner_axis)
        if exact:
            total = dot(a[0], wide, dims)
        elif inner <= TILE:
            both = jnp.concatenate([wide, wide], axis=inner_axis)
            total = dot(jnp.concatenate(a, axis=1), both, dims)
        else:
            total = dot(a[0], wide, dims) + dot(a[1], wide, dims)
        return total[:, :outer] + total[:, outer:]
    if inner <= TILE:
        if exact:
            deep = jnp.concatenate([high, low], axis=inner_axis)
            return dot(jnp.concatenate([a[0], a[0]], axis=1), deep, dims)
        deep = jnp.concatenate([high, high], axis=inner_axis)
        return dot(jnp.concatenate(a, axis=1), deep, dims) + dot(a[0], low, dims)
    total = dot(a[0], high, dims) + dot(a[0], low, dims)
    return total if exact else total + dot(a[1], high, dims)


def together(works):
    works = list(works)
    while works:
        works = [work for work in works if next(work, works) is None]
        yield


def finish(work):
    for _ in work:
        pass


def iotas(rows, cols):
    return (
        lax.broadcasted_iota(jnp.int32, (rows, cols), 0),
        lax.broadcasted_iota(jnp.int32, (rows, cols), 1),
    )


def tile_inverses(lowers):
    row, col = iotas(TILE, TILE)
    eye = jnp.where(row == col, 1.0, 0.0).astype(f32)
    width = BASE
    same = row // width == col // width
    inverses = [eye - jnp.where(same, low, 0.0) for low in lowers]
    while width < TILE:
        same = row // width == col // width
        wider = row // (2 * width) == col // (2 * width)
        between = wider & jnp.logical_not(same)
        parts = [split(inv) for inv in inverses]
        inner = [
            mm(split(jnp.where(between, low, 0.0)), inv) for low, inv in zip(lowers, parts)
        ]
        inverses = [inv - mm(p, split(i)) for inv, p, i in zip(inverses, parts, inner)]
        width *= 2
    return inverses


def unit_lower_inverses(lowers):
    size = lowers[0].shape[0]
    if size == TILE:
        return tile_inverses(lowers)
    half = size // 2
    inverses = unit_lower_inverses(
        [low[:half, :half] for low in lowers] + [low[half:, half:] for low in lowers]
    )
    first, second = (inverses[: len(lowers)], inverses[len(lowers) :])
    inner = [mm(split(low[half:, :half]), split(inv)) for low, inv in zip(lowers, first)]
    below = [-mm(split(inv), split(i)) for inv, i in zip(second, inner)]
    zero = jnp.zeros((half, half), f32)
    return [
        jnp.concatenate(
            [jnp.concatenate([a, zero], axis=1), jnp.concatenate([c, b], axis=1)], axis=0
        )
        for a, b, c in zip(first, second, below)
    ]


def sigmoid(a):
    return 1.0 / (1.0 + jnp.exp(-a))


def unit_rows(a):
    scale = lax.rsqrt(jnp.sum(a * a, axis=-1, keepdims=True) + norm_eps)
    return (a * scale, scale)


def prefix_sums(a):
    count, size = a.shape
    high, low = split(a)
    rest = (a - high.astype(f32) - low.astype(f32)).astype(bf16)
    row, col = iotas(size, size)
    parts = dot(
        jnp.concatenate([high, low, rest], axis=0), jnp.where(row <= col, 1.0, 0.0).astype(bf16), NN
    )
    return parts[:count] + parts[count : 2 * count] + parts[2 * count :]


def gates_kernel(
    place_ref, logit_ref, decay_ref, mixed_ref, w_ref, do_ref,
    causal_ref, gates_ref, beta_ref, own_ref, w_out, do_out,
):
    own_ref[...] = mixed_ref[:, lanes(place_ref[0] * own_ref.shape[1], own_ref.shape[1])]
    w_out[...] = w_ref[...]
    do_out[...] = do_ref[...]
    heads, tokens = decay_ref.shape
    row, col = iotas(tokens, tokens)
    cum = prefix_sums(decay_ref[...])
    beta = sigmoid(logit_ref[...])
    beta_ref[...] = beta
    cols = jnp.concatenate([cum, beta], axis=0).T
    for g in range(heads // RATIO):
        first = g * RATIO
        for h in range(first, first + RATIO):
            ratio = jnp.exp(jnp.minimum(cols[:, h : h + 1] - cum[h : h + 1], 0.0))
            causal_ref[h] = jnp.where(col <= row, ratio, 0.0)
        cum_c = cols[:, first : first + RATIO]
        gates_ref[g, :, :RATIO] = cols[:, heads + first : heads + first + RATIO]
        gates_ref[g, :, RATIO : 2 * RATIO] = jnp.exp(cum_c)
        gates_ref[g, :, 2 * RATIO : 3 * RATIO] = jnp.exp(cum_c[tokens - 1 :] - cum_c)


def wide_gates(gates_ref, group, h):
    tokens = gates_ref.shape[1]
    cols = [gates_ref[group, :, i * RATIO + h : i * RATIO + h + 1] for i in range(3)]
    return [jnp.broadcast_to(c, (tokens, DK)) for c in cols]


def group_at(place_ref, slot):
    first, flip = slot
    return first if flip is None else first + ((place_ref[1] & 1) ^ flip)


def lanes(start, size):
    return pl.ds(start if isinstance(start, int) else pl.multiple_of(start, size), size)


def local_kernel(slots, place_ref, *refs):
    each = len(slots)
    outs, exts = (refs[-6 * each : -each], refs[-each:])
    groups = [group_at(place_ref, slot) for slot in slots]
    lowers = []
    for at, group in enumerate(groups):
        lowers += group_system(
            group, place_ref, refs[: -6 * each], *outs[at : 3 * each : each], exts[at]
        )
    inverses = unit_lower_inverses(lowers)
    for at, group in enumerate(groups):
        finish(
            group_maps(
                group, inverses[at * RATIO : (at + 1) * RATIO], refs[: -6 * each],
                *outs[each + at :: each],
            )
        )


def group_system(group, place_ref, refs, x_out, act_ref, slope_ref, ext):
    *piece_refs, halo_ref, w_ref, causal_ref, gates_in, do_ref = refs
    mine = place_ref[0]
    here = lanes(group * GROUP, GROUP)
    count = piece_refs[0].shape[0]
    pieces = len(piece_refs)
    tokens = pieces * count
    ext[:EDGE] = halo_ref[:, here].astype(f32)
    x_out[:EDGE] = halo_ref[:, here]
    for s in range(pieces):
        piece = piece_refs[s][:, here]
        begin = pl.multiple_of(EDGE + (mine ^ s) * count, EDGE)
        ext[pl.ds(begin, count)] = piece.astype(f32)
        x_out[pl.ds(begin, count)] = piece
    start = EDGE - (KW - 1)
    conv = w_ref[0:1, here] * ext[start : start + tokens]
    for tap in range(1, KW):
        conv += w_ref[tap : tap + 1, here] * ext[start + tap : start + tap + tokens]
    gate = sigmoid(conv)
    act = conv * gate
    slope = gate + act * (1.0 - gate)
    qn, q_scale = unit_rows(act[:, :DK])
    k, k_scale = unit_rows(act[:, DK : 2 * DK])
    act_ref[:, :DK] = qn
    act_ref[:, DK : 2 * DK] = k
    act_ref[:, 2 * DK :] = act[:, 2 * DK :]
    slope_ref[:, :DK] = slope[:, :DK] * q_scale
    slope_ref[:, DK : 2 * DK] = slope[:, DK : 2 * DK] * k_scale
    slope_ref[:, 2 * DK :] = slope[:, 2 * DK :]
    ks = split(k)
    gram = mm(ks, ks, NT)
    row, col = iotas(tokens, tokens)
    gram = jnp.where(col < row, gram, 0.0)
    lowers = []
    for h in range(RATIO):
        beta = wide_gates(gates_in, group, h)[0]
        wide = jnp.concatenate([beta] * (tokens // DK), axis=1)
        lowers.append(causal_ref[group * RATIO + h] * gram * wide)
    return lowers


def group_maps(group, inverses, refs, act_ref, slope_ref, saved_ref, maps_ref):
    *_, causal_ref, gates_in, do_ref = refs
    tokens = act_ref.shape[0]
    q = act_ref[:, :DK] * DK**-0.5
    k = act_ref[:, DK : 2 * DK]
    scores = mm(split(q), split(k), NT)
    qt = split(q.T)
    kt = split(k.T)
    yield

    def head_maps(h):
        head = group * RATIO + h
        beta, gamma, tail = wide_gates(gates_in, group, h)
        beta_gamma = beta * gamma
        v = act_ref[:, 2 * DK + h * DV : 2 * DK + (h + 1) * DV]
        do = do_ref[:, lanes(head * DV, DV)]
        solved = mm(split(inverses[h]), split(jnp.concatenate([beta * v, beta_gamma * k], axis=1)))
        du = mm(split((causal_ref[head] * scores).T), (do,))
        yield
        saved_ref[h, :, : DV + DK] = solved
        pulled = mm(split(inverses[h].T), split(jnp.concatenate([du, tail * k], axis=1)))
        yield
        saved_ref[h, :, DV + DK :] = pulled
        packed = [tail * solved[:, :DV], tail * solved[:, DV:], beta_gamma * pulled[:, :DV]]
        moved = mm(kt, split(jnp.concatenate(packed, axis=1)))
        adjoint = mm(qt, split(gamma * do.astype(f32)))
        yield
        drow, dcol = iotas(DK, DK)
        total = gamma[tokens - 1 :]
        maps_ref[h, 0] = jnp.where(drow == dcol, total, 0.0) - moved[:, DV : DV + DK]
        maps_ref[h, 1] = moved[:, :DV]
        maps_ref[h, 2] = adjoint - moved[:, DV + DK :]

    yield from together(head_maps(h) for h in range(RATIO))


def ordered(core, own, other):
    return (jnp.where(core == 0, own, other), jnp.where(core == 0, other, own))


def compose_kernel(parts, place_ref, *refs):
    keeps, others, outs, held = (refs[:parts], refs[parts : 2 * parts], refs[2 * parts : -1], refs[-1])
    core, chip = (place_ref[1] & 1, place_ref[1] >> 1)
    share = keeps[0].shape[0]
    for p in range(parts):
        for i in range(share):
            maps0, maps1 = ordered(core, keeps[p][i], others[p][i])
            later = mm(split(maps1[0]), split(jnp.concatenate([maps0[0], maps0[1]], axis=1)))
            held[p * share + i, 0] = later[:, :DK]
            held[p * share + i, 1] = later[:, DK:] + maps1[1]
            held[p * share + i, 2] = mm(split(maps0[0].T), split(maps1[2])) + maps0[2]
    for s, out in enumerate(outs):
        out[...] = held[chip ^ s]


def chips_kernel(chips, place_ref, *refs):
    maps_refs, first_ref, last_ref, outs, held, ends = (
        refs[:chips], refs[chips], refs[chips + 1], refs[chips + 2 : -2], refs[-2], refs[-1],
    )
    chip = place_ref[1] >> 1
    for s, maps_ref in enumerate(maps_refs):
        held[chip ^ s] = maps_ref[...]
    share = RATIO
    head = (chip // share * 2 + (place_ref[1] & 1)) * share + chip % share
    state, adjoint = (first_ref[head], last_ref[head])
    for step in range(chips):
        back = chips - 1 - step
        ends[step, 0] = state
        ends[back, 1] = adjoint
        if step < chips - 1:
            state = mm(split(held[step, 0]), split(state)) + held[step, 1]
            adjoint = mm(split(held[back, 0].T), split(adjoint)) + held[back, 2]
    for s, out in enumerate(outs):
        out[...] = ends[chip ^ s]


def expand_kernel(chips, place_ref, *refs):
    ends_refs, refs = (refs[:chips], refs[chips:])
    *maps_refs, own_out, give_out, ends = refs
    parts = len(maps_refs) // 2
    keeps, others = (maps_refs[:parts], maps_refs[parts:])
    core, chip = (place_ref[1] & 1, place_ref[1] >> 1)
    for s, ends_ref in enumerate(ends_refs):
        ends[chip ^ s] = ends_ref[...]
    share = keeps[0].shape[0]
    for p in range(parts):
        for i in range(share):
            head = p * share + i
            state, adjoint = (ends[head, 0], ends[head, 1])
            maps0, maps1 = ordered(core, keeps[p][i], others[p][i])
            state1 = mm(split(maps0[0]), split(state)) + maps0[1]
            adjoint0 = mm(split(maps1[0].T), split(adjoint)) + maps1[2]
            own_out[head, 0], give_out[head, 0] = ordered(core, state, state1)
            own_out[head, 1], give_out[head, 1] = ordered(core, adjoint0, adjoint)


def scan_kernel(maps_ref, first_ref, last_ref, out_ref):
    count = maps_ref.shape[0]
    state, adjoint = (first_ref[0], last_ref[0])
    for step in range(count):
        back = count - 1 - step
        out_ref[step, 0, 0] = state
        out_ref[back, 0, 1] = adjoint
        if step < count - 1:
            state = mm(split(maps_ref[step, 0, 0]), split(state)) + maps_ref[step, 0, 1]
            adjoint = mm(split(maps_ref[back, 0, 0].T), split(adjoint)) + maps_ref[back, 0, 2]


def row_sums(a):
    return dot(jnp.ones((8, 2 * DK), bf16), jnp.concatenate(split(a), axis=1), NT)[:1]


def wide_row_sums(a):
    return dot(jnp.concatenate(split(a), axis=1), jnp.ones((2 * DK, DK), bf16), NN)


def grad_kernel(slots, sides, place_ref, *refs):
    each = len(slots)
    w_ref, beta_ref, causal_ref, gates_in, do_ref, *refs = refs
    ends_refs, refs = (refs[:sides], refs[sides:])
    kept, (*out_refs, dext, ext) = (refs[: 4 * each], refs[4 * each :])
    out_refs, last_refs = (out_refs[:-5], out_refs[-5:])
    works = []
    for at, slot in enumerate(slots):
        side, first = divmod(at * RATIO, each * RATIO // sides)
        works.append(
            group_grads(
                group_at(place_ref, slot), at, place_ref[0], *kept[4 * at : 4 * at + 4], w_ref,
                beta_ref, causal_ref, gates_in, do_ref, ends_refs[side].at[pl.ds(first, RATIO)],
                out_refs, *last_refs, dext.at[at % STEP], ext.at[at % STEP],
            )
        )
    for first in range(0, each, STEP):
        finish(together(works[first : first + STEP]))


def group_grads(
    group, at, mine, x_ref, act_ref, slope_ref, saved_ref, w_ref, beta_ref, causal_ref, gates_in,
    do_ref, ends_ref, out_refs, edge_ref, spill_ref, dw_ref, decay_ref, logit_ref, dext, ext,
):
    tokens = act_ref.shape[0]
    here = lanes(group * GROUP, GROUP)
    there = slice(at * GROUP, (at + 1) * GROUP)
    qn = act_ref[:, :DK]
    q = qn * DK**-0.5
    k = act_ref[:, DK : 2 * DK]
    qs, ks = (split(q), split(k))
    gram = mm(ks, ks, NT)
    scores = mm(qs, ks, NT)
    row, col = iotas(tokens, tokens)
    below = col < row
    suffix = jnp.where(row >= col, 1.0, 0.0).astype(bf16)
    yield
    results = [None] * RATIO

    def head_grads(h):
        head = group * RATIO + h
        beta, gamma, tail = wide_gates(gates_in, group, h)
        v = act_ref[:, 2 * DK + h * DV : 2 * DK + (h + 1) * DV]
        do = (do_ref[:, lanes(head * DV, DV)],)
        state, adjoint = (ends_ref[h, 0], ends_ref[h, 1])
        ss, ds = (split(state), split(adjoint))
        u = saved_ref[h, :, :DV] - mm(split(saved_ref[h, :, DV : DV + DK]), ss)
        z = saved_ref[h, :, DV + DK : 2 * DV + DK] + mm(
            split(saved_ref[h, :, 2 * DV + DK :]), ds
        )
        yield
        dv = beta * z
        us, zs = (split(u), split(dv))
        dq_in = gamma * mm(do, ss, NT)
        dk_in = gamma * mm(zs, ss, NT)
        dk_out = tail * mm(us, ds, NT)
        yield
        causal = causal_ref[head]
        score_part = mm(do, us, NT) * causal
        gram_part = jnp.where(below, mm(zs, us, NT) * causal, 0.0)
        yield
        gram_term = gram_part * gram
        both = score_part * scores - gram_term
        key_in = dk_in * k
        left = dk_out * k
        parts = both[:, :DK]
        terms = gram_term[:, :DK]
        for begin in range(DK, tokens, DK):
            parts += both[:, begin : begin + DK]
            terms += gram_term[:, begin : begin + DK]
        dcum = row_sums(parts + dq_in * q - key_in - left) - jnp.sum(both, axis=0, keepdims=True)
        results[h] = (dq_in, dk_out - dk_in, dv, score_part, gram_part)
        yield
        high, low = split(dcum)
        rest = (dcum - high.astype(f32) - low.astype(f32)).astype(bf16)
        stack = [high, low, rest, high, low, rest, high, low]
        summed = dot(jnp.concatenate(stack, axis=0), suffix, NN)
        at_end = jnp.sum(left, axis=0, keepdims=True) + gamma[tokens - 1 :] * jnp.sum(
            state * adjoint, axis=0, keepdims=True
        )
        decay_ref[pl.ds(head, 1)] = (
            summed[0:1] + summed[1:2] + summed[2:3] + jnp.sum(at_end, axis=1, keepdims=True)
        )
        closed = 1.0 - beta_ref[pl.ds(head, 1)]
        logit_ref[pl.ds(head, 1)] = closed * row_sums(dv * v - terms - key_in)

    yield from together(head_grads(h) for h in range(RATIO))
    dq, dk, _, dscores, dgram = (sum(parts[1:], parts[0]) for parts in zip(*results))
    dgram = -dgram
    dvs = [result[2] for result in results]
    dss, dgs = (split(dscores), split(dgram + dgram.T))
    dq += mm(dss, ks)
    dk += mm(split(dscores.T), qs) + mm(dgs, ks)
    yield
    dq *= DK**-0.5
    dconv = jnp.concatenate(
        [dq - qn * wide_row_sums(qn * dq), dk - k * wide_row_sums(k * dk)] + dvs, axis=1
    )
    dconv *= slope_ref[...]
    ext[...] = x_ref[...].astype(f32)
    start = EDGE - (KW - 1)
    for tap in range(KW):
        dw_ref[tap : tap + 1, here] = jnp.sum(
            dconv * ext[start + tap : start + tap + tokens], axis=0, keepdims=True
        )
    zero = jnp.zeros((EDGE, GROUP), f32)
    yield
    dext[:EDGE] = zero
    dext[EDGE : EDGE + tokens] = dconv
    dext[EDGE + tokens :] = zero
    own = jnp.zeros((tokens, GROUP), f32)
    spill = jnp.zeros((EDGE, GROUP), f32)
    for tap in range(KW):
        begin = EDGE + KW - 1 - tap
        own += w_ref[tap : tap + 1, here] * dext[begin : begin + tokens]
        begin = KW - 1 - tap
        spill += w_ref[tap : tap + 1, here] * dext[begin : begin + EDGE]
    ext[:tokens] = own
    count = tokens // len(out_refs)
    for s, out_ref in enumerate(out_refs):
        begin = pl.multiple_of((mine ^ s) * count, EDGE)
        out_ref[:, there] = ext[pl.ds(begin, count)].astype(bf16)
    edge_ref[:, here] = own[tokens - EDGE :]
    spill_ref[:, here] = spill


def pack_kernel(place_ref, mixed_ref, *outs):
    feats = mixed_ref.shape[1] // (len(outs) + 1)
    for s, out in enumerate(outs):
        out[...] = mixed_ref[:, lanes((place_ref[0] ^ (s + 1)) * feats, feats)]


def assemble_kernel(slots, place_ref, *refs):
    *refs, out_ref = refs
    pieces = len(refs) // 2
    rows = out_ref.shape[0]
    feats = out_ref.shape[1] // pieces
    for at, slot in enumerate(slots):
        for s in range(pieces):
            begin = (place_ref[0] ^ s) * feats + group_at(place_ref, slot) * GROUP
            out_ref[:, lanes(begin, GROUP)] = refs[s][:, at * GROUP : (at + 1) * GROUP]

    @pl.when(place_ref[0] == pieces - 1)
    def fix():
        for s in range(pieces):
            out_ref[rows - EDGE :, s * feats : (s + 1) * feats] = refs[pieces + s][...]


def shape(*dims, dtype=f32):
    return jax.ShapeDtypeStruct(dims, dtype)


def call(kernel, name, out_shape, place, args, scratch=(), flops=0):
    vmem = pl.BlockSpec(memory_space=pltpu.VMEM)
    return pl.pallas_call(
        kernel,
        in_specs=[pl.BlockSpec(memory_space=pltpu.SMEM)] + [vmem] * len(args),
        out_specs=jax.tree.map(lambda _: vmem, out_shape),
        out_shape=out_shape,
        scratch_shapes=scratch,
        compiler_params=pltpu.CompilerParams(vmem_limit_bytes=VMEM_BYTES),
        cost_estimate=pl.CostEstimate(flops=flops, bytes_accessed=1 << 20, transcendentals=0),
        name=name,
    )(place, *args)


def from_behind(value, axis, by):
    devices = lax.axis_size(axis)
    pairs = [(i, i + by) for i in range(devices) if 0 <= i + by < devices]
    return lax.ppermute(value, axis, pairs)


def across(value, axis, by):
    return lax.ppermute(value, axis, [(i, i ^ by) for i in range(lax.axis_size(axis))])


def local_pass(place, slots, received, halo, weight, gates, do):
    tokens = gates[0].shape[1]
    each = len(slots)
    outs = call(
        functools.partial(local_kernel, slots),
        "local_pass",
        [shape(EDGE + tokens, GROUP, dtype=bf16)] * each
        + [shape(tokens, GROUP)] * (2 * each)
        + [shape(RATIO, tokens, 2 * (DV + DK))] * each
        + [shape(RATIO, 3, DK, DV)] * each,
        place,
        [*received, halo, weight, *gates, do],
        [pltpu.VMEM((EDGE + tokens, GROUP), f32)] * each,
        flops=each * 6 * 10**9,
    )
    kept = [outs[at : 4 * each : each] for at in range(each)]
    return (kept, outs[4 * each :])


def grad_pass(place, slots, kept, ends, weight, beta, gates, do, pieces):
    tokens = do.shape[0]
    each = len(slots)
    outs = call(
        functools.partial(grad_kernel, slots, len(ends)),
        "grad_pass",
        [shape(tokens // pieces, each * GROUP, dtype=bf16)] * pieces
        + [
            shape(EDGE, each * GROUP),
            shape(EDGE, each * GROUP),
            shape(KW, each * GROUP),
            shape(each * RATIO, tokens),
            shape(each * RATIO, tokens),
        ],
        place,
        [weight, beta, *gates, do, *ends, *[a for part in kept for a in part]],
        [
            pltpu.VMEM((STEP, tokens + 2 * EDGE, GROUP), f32),
            pltpu.VMEM((STEP, tokens + EDGE, GROUP), f32),
        ],
        flops=each * 4 * 10**9,
    )
    return (outs[:pieces], *outs[pieces:])


def scan_pass(maps, first, last):
    count, heads = maps.shape[:2]
    return pl.pallas_call(
        scan_kernel,
        grid=(heads,),
        in_specs=[
            pl.BlockSpec((count, 1, 3, DK, DV), lambda h: (0, h, 0, 0, 0)),
            pl.BlockSpec((1, DK, DV), lambda h: (h, 0, 0)),
            pl.BlockSpec((1, DK, DV), lambda h: (h, 0, 0)),
        ],
        out_specs=pl.BlockSpec((count, 1, 2, DK, DV), lambda h: (0, h, 0, 0, 0)),
        out_shape=shape(count, heads, 2, DK, DV),
        compiler_params=pltpu.CompilerParams(vmem_limit_bytes=4 * VMEM_BYTES),
        name="scan_pass",
    )(maps, first, last)


def cross_chips(place, keeps, others, initial_state, final_state_grad):
    parts = len(keeps)
    chips = parts * keeps[0].shape[0]
    joined = call(
        functools.partial(compose_kernel, parts),
        "join_cores",
        [shape(3, DK, DV)] * chips,
        place,
        [*keeps, *others],
        [pltpu.VMEM((chips, 3, DK, DV), f32)],
    )
    held = [joined[0]] + [across(joined[s], "ctx", 2 * s) for s in range(1, chips)]
    ends = call(
        functools.partial(chips_kernel, chips),
        "over_chips",
        [shape(2, DK, DV)] * chips,
        place,
        [*held, initial_state, final_state_grad],
        [pltpu.VMEM((chips, 3, DK, DV), f32), pltpu.VMEM((chips, 2, DK, DV), f32)],
    )
    ends = [ends[0]] + [across(ends[s], "ctx", 2 * s) for s in range(1, chips)]
    own, give = call(
        functools.partial(expand_kernel, chips),
        "within_chip",
        [shape(chips, 2, DK, DV)] * 2,
        place,
        [*ends, *keeps, *others],
        [pltpu.VMEM((chips, 2, DK, DV), f32)],
    )
    return (own, across(give, "ctx", 1))


def on_device(
    mixed_in,
    conv_weight,
    write_strength_logit,
    decay_log,
    initial_state,
    final_state_grad,
    grad_out,
):
    devices, pieces = (lax.axis_size("ctx"), lax.axis_size("head"))
    heads, tokens = decay_log.shape
    groups = heads // RATIO
    feats = groups * GROUP
    paired = heads == devices and groups == 4
    slots = tuple((g, None) for g in range(groups))
    if paired:
        slots = tuple((g, flip) for flip in (1, 0) for g in range(0, groups, 2))
    place = jnp.stack([lax.axis_index("head"), lax.axis_index("ctx")]).astype(jnp.int32)
    packed = call(
        pack_kernel,
        "pack",
        [shape(mixed_in.shape[0], feats, dtype=bf16)] * (pieces - 1),
        place,
        [mixed_in],
    )
    arrived = [across(piece, "head", s + 1) for s, piece in enumerate(packed)]
    causal, gates, beta, own_piece, near_weight, near_do = call(
        gates_kernel,
        "gates_pass",
        [
            shape(heads, tokens, tokens),
            shape(groups, tokens, 8),
            shape(heads, tokens),
            shape(mixed_in.shape[0], feats, dtype=bf16),
            shape(*conv_weight.shape),
            shape(*grad_out.shape, dtype=bf16),
        ],
        place,
        [write_strength_logit, decay_log, mixed_in, conv_weight, grad_out],
    )
    arrived[0], own_piece = lax.optimization_barrier((arrived[0], own_piece))
    arrived = [own_piece, *arrived]
    gates = (causal, gates)
    mine = lax.axis_index("head")
    edge_rows = own_piece[own_piece.shape[0] - EDGE :]
    for s in range(1, pieces):
        edge_rows = jnp.where((mine ^ s) == pieces - 1, arrived[s][-EDGE:], edge_rows)
    halo = from_behind(edge_rows, "ctx", 1)
    kept, maps = local_pass(place, slots, arrived, halo, near_weight, gates, near_do)
    if paired:
        others = [across(part, "ctx", 1) for part in maps[: groups // 2]]
        own_ends, other_ends = cross_chips(
            place, maps[groups // 2 :], others, initial_state, final_state_grad
        )
        ends = [other_ends, own_ends]
    else:
        gathered = lax.all_gather(jnp.concatenate(maps), "ctx")
        gathered = scan_pass(gathered, initial_state, final_state_grad)
        ends = [lax.dynamic_index_in_dim(gathered, lax.axis_index("ctx"), 0, keepdims=False)]
    out_pieces, edge, spill, dweight, grad_decay, grad_beta = grad_pass(
        place, slots, kept, ends, conv_weight, beta, gates, grad_out, pieces
    )
    received = [out_pieces[0]] + [across(out_pieces[s], "head", s) for s in range(1, pieces)]
    spilled, dweight = lax.optimization_barrier((from_behind(spill, "ctx", -1), dweight))
    last = (edge + spilled).astype(bf16)
    last_rows = [
        lax.ppermute(
            last, ("ctx", "head"), [(c * pieces + h, (c + 1) * pieces - 1) for c in range(devices)]
        )
        for h in range(pieces - 1)
    ] + [last]
    returned = call(
        functools.partial(assemble_kernel, slots),
        "assemble",
        shape(mixed_in.shape[0], feats * pieces, dtype=bf16),
        place,
        [*received, *last_rows],
    )
    if devices & (devices - 1) == 0:
        by = 1
        while by < devices:
            dweight = dweight + across(dweight, "ctx", by)
            by *= 2
    else:
        dweight = lax.psum(dweight, "ctx")
    return (returned, dweight, grad_beta, grad_decay)


def solution(mesh):
    in_specs = (
        P(("ctx", "head"), None),
        P(None, "head"),
        P("head", "ctx"),
        P("head", "ctx"),
        P("head", None, None),
        P("head", None, None),
        P("ctx", "head"),
    )
    out_specs = (P(("ctx", "head"), None), P(None, "head"), P("head", "ctx"), P("head", "ctx"))
    return jax.shard_map(
        on_device, mesh=mesh, in_specs=in_specs, out_specs=out_specs, check_vma=False
    )
```
